256 devices in a mesh: row: 8 (over z_hi, core), col: 32 (over x, z_lo, y).
Axes of the slice: x: 4, y: 4, z: 8 (z_hi: 4, z_lo: 2; z = z_hi * 2 + z_lo), core: 2. Of those that a mesh axis runs over, the one named last changes fastest.
Arguments:
- features: bfloat16 [8, 32, 1024, 512], P('row', 'col'), may hold values from -64 to 64
- values: bfloat16 [8, 32, 1024, 512], P('row', 'col'), may hold values from -6 to 6
- out_grad: bfloat16 [8, 32, 1024, 512], P('row', 'col'), may hold values from -6 to 6
- query_weight: float32 [8, 32, 512, 512], P('row', 'col'), may hold values from -6 to 6
- key_weight: float32 [8, 32, 512, 512], P('row', 'col'), may hold values from -6 to 6
- query_mean: float32 [8, 32, 512, 512], P('row', 'col'), may hold values from -0.3 to 0.3
- query_square: float32 [8, 32, 512, 512], P('row', 'col'), may hold values from 0.001 to 0.01
- key_mean: float32 [8, 32, 512, 512], P('row', 'col'), may hold values from -0.3 to 0.3
- key_square: float32 [8, 32, 512, 512], P('row', 'col'), may hold values from 0.001 to 0.01
- members: int32 [8, 32, 2], P('row', 'col'), may hold values 0 or 1
Outputs:
- query_result: float32 [8, 32, 512, 512], P('row', 'col')
- key_result: float32 [8, 32, 512, 512], P('row', 'col')
The draws below stay inside these ranges and needn't reach their ends.
All inputs are finite; a program needn't handle non-finite values. No bound on the sum of `members` on one device may be relied on, other than what follows from the above.
Results may differ from the reference program's by a relative error of at most 0.023.
The reference program's roundings to bfloat16 on the way count: a program that leaves them out, or rounds other values in their place, can miss the bound.
Values sent between devices are 32-bit elements; how exact they have to be, the bound alone decides.
No kernel may reach another device: no remote copies, remote signals or barrier semaphores. Data moves between devices by JAX's collectives and lax.ppermute only.
A program may use at most 64 MiB of HBM per device.

```python
import math
import jax
import jax.numpy as jnp
from jax import lax

DW = 512
HD = 64
SEQ = 512
TOK = 1024
HW = 512
GROUP_ROW = 4
GROUP_COL = 4
N_ROW = 8
N_COL = 32


def draw_features(key, part):
    key = jax.random.fold_in(key, 7)
    base = jax.random.normal(key, (N_ROW, N_COL, TOK, DW), jnp.float32)
    return jnp.clip(base, -64.0, 64.0).astype(jnp.bfloat16)


def set_ends(values, key, smallest, top_value):
    shape = values.shape
    index_at = [jax.random.randint(jax.random.fold_in(key, axis), (), 0, shape[axis]) for axis in range(len(shape))]
    values = values.at[tuple(index_at)].set(smallest)
    longest = shape.index(max(shape))
    index_at[longest] = (index_at[longest] + 1) % shape[longest]
    return values.at[tuple(index_at)].set(top_value)


def level_of(key, extent, pieces, low, high):
    loudness = 1.0
    for axis_at, parts in pieces:
        steps = jax.random.uniform(jax.random.fold_in(jax.random.fold_in(key, 6), axis_at), (parts,), jnp.float32, low / len(pieces), high / len(pieces))
        loudness = loudness * jnp.repeat(jnp.exp(steps), extent[axis_at] // parts).reshape((-1,) + (1,) * (len(extent) - 1 - axis_at))
    return loudness


def noise(key, shape, scale, reach, pieces=(), held_as=jnp.bfloat16):
    factor_of = level_of(key, shape, pieces, -0.22, 0.18) if pieces else 1.0
    values = jax.random.normal(key, shape, jnp.float32) * scale * factor_of
    return jnp.minimum(jnp.maximum(values, -reach), reach).astype(held_as)


def setup_inputs(seed: int = 0) -> dict:
    seeds = jax.random.split(jax.random.key(seed), 11)
    return {
        "features": draw_features(jax.random.fold_in(seeds[10], 71), 0),
        "values": noise(seeds[1], (N_ROW, N_COL, TOK, HW), 1.0, 6.0, ((0, 8), (1, 32))),
        "out_grad": noise(seeds[2], (N_ROW, N_COL, TOK, HW), 1.0, 6.0, ((0, 8), (1, 32))),
        "query_weight": noise(seeds[3], (N_ROW, N_COL, DW, HW), 1.0, 6.0, ((0, 8), (1, 32)), jnp.float32),
        "key_weight": noise(seeds[4], (N_ROW, N_COL, DW, HW), 1.0, 6.0, ((0, 8), (1, 32)), jnp.float32),
        "query_mean": noise(seeds[5], (N_ROW, N_COL, DW, HW), 0.05, 0.3, ((0, 8), (1, 32)), jnp.float32),
        "query_square": jnp.clip(jnp.exp(math.log(0.01) - 2.30258502 * jax.random.uniform(seeds[6], (N_ROW, N_COL, DW, HW), jnp.float32) ** level_of(seeds[6], (N_ROW, N_COL, DW, HW), ((0, 8), (1, 32)), -0.2, 0.2)), 0.001, 0.01),
        "key_mean": noise(seeds[7], (N_ROW, N_COL, DW, HW), 0.05, 0.3, ((0, 8), (1, 32)), jnp.float32),
        "key_square": jnp.clip(jnp.exp(math.log(0.01) - 2.30258502 * jax.random.uniform(seeds[8], (N_ROW, N_COL, DW, HW), jnp.float32) ** level_of(seeds[8], (N_ROW, N_COL, DW, HW), ((0, 8), (1, 32)), -0.2, 0.2)), 0.001, 0.01),
        "members": set_ends((jax.random.randint(seeds[9], (N_ROW, N_COL, 2), 0, 4) < 3).astype(jnp.int32), jax.random.fold_in(seeds[9], 1), 0, 1),
    }


beta_one = 0.9
beta_two = 0.999
epsilon = 1e-06
decay_rate = 0.01
learn_rate = 0.1
correction_one = 1.0 - math.exp(100.0 * math.log(0.9))
correction_two = 1.0 - math.exp(100.0 * math.log(0.999))

def rounded(array):
    return lax.optimization_barrier(array.astype(jnp.bfloat16)).astype(jnp.float32)

def attend_back(seq_block):
    queries, key_rows, value_rows, grad_rows = seq_block
    length = queries.shape[0]
    head_count = queries.shape[1] // HD
    score_scale = 1.0 / math.sqrt(HD)
    query_heads = queries.reshape(length, head_count, HD).astype(jnp.float32)
    key_heads = key_rows.reshape(length, head_count, HD).astype(jnp.float32)
    value_heads = value_rows.reshape(length, head_count, HD).astype(jnp.float32)
    grad_heads = grad_rows.reshape(length, head_count, HD).astype(jnp.float32)
    scores = jnp.einsum('qhd,khd->hqk', query_heads, key_heads) * score_scale
    highest = lax.optimization_barrier(jnp.max(scores, axis=-1, keepdims=True))
    exponent = jnp.exp(scores - highest)
    softmax_out = exponent / lax.optimization_barrier(jnp.sum(exponent, axis=-1, keepdims=True))
    prob_low = rounded(softmax_out)
    output = jnp.einsum('hqk,khd->qhd', prob_low, value_heads)
    grad_prob = jnp.einsum('qhd,khd->hqk', grad_heads, value_heads)
    row_delta = jnp.transpose(lax.optimization_barrier(jnp.sum(grad_heads * output, axis=-1)))[:, :, None]
    grad_score = rounded(softmax_out * (grad_prob - row_delta) * score_scale)
    grad_query = jnp.einsum('hqk,khd->qhd', grad_score, key_heads).astype(jnp.bfloat16)
    grad_key = jnp.einsum('hqk,qhd->khd', grad_score, query_heads).astype(jnp.bfloat16)
    return (grad_query.reshape(length, -1), grad_key.reshape(length, -1))

def lamb_update(weight, first, second, grad):
    first_new = beta_one * first + (1.0 - beta_one) * grad
    second_new = beta_two * second + (1.0 - beta_two) * grad * grad
    update = first_new / correction_one / (jnp.sqrt(second_new / correction_two) + epsilon) + decay_rate * weight
    ratio = jnp.sqrt(jnp.sum(weight * weight)) / jnp.sqrt(jnp.sum(update * update) + epsilon)
    return weight - learn_rate * ratio * update

def replica_step(replica_in):
    feature_rows, value_rows, grad_rows, query_w, key_w, query_m, query_s, key_m, key_s = replica_in
    in_scale = 1.0 / math.sqrt(feature_rows.shape[1])
    queries = (jnp.dot(feature_rows, query_w.astype(jnp.bfloat16), preferred_element_type=jnp.float32) * in_scale).astype(jnp.bfloat16)
    key_rows = (jnp.dot(feature_rows, key_w.astype(jnp.bfloat16), preferred_element_type=jnp.float32) * in_scale).astype(jnp.bfloat16)
    seq_count = feature_rows.shape[0] // SEQ

    def by_sequence(array):
        return array.reshape(seq_count, SEQ, array.shape[-1])
    grad_query, grad_key = lax.map(attend_back, (by_sequence(queries), by_sequence(key_rows), by_sequence(value_rows), by_sequence(grad_rows)))
    feature_wide = feature_rows.astype(jnp.float32)
    query_grad = jnp.einsum('td,th->dh', feature_wide, grad_query.reshape(-1, grad_query.shape[-1]).astype(jnp.float32)) * in_scale
    key_grad = jnp.einsum('td,th->dh', feature_wide, grad_key.reshape(-1, grad_key.shape[-1]).astype(jnp.float32)) * in_scale
    return (lamb_update(query_w, query_m, query_s, query_grad), lamb_update(key_w, key_m, key_s, key_grad))

def group_mean(stacked, active, group_size):
    row_total = stacked.shape[0]
    inner = stacked.shape[1:]
    weighted = stacked * active[:, :, None, None]
    summed = lax.optimization_barrier(jnp.sum(weighted.reshape((row_total // group_size, group_size) + inner), axis=1, keepdims=True))
    summed = jnp.broadcast_to(summed, (row_total // group_size, group_size) + inner).reshape(stacked.shape)
    counts = lax.optimization_barrier(jnp.sum(active.reshape(row_total // group_size, group_size, active.shape[1]), axis=1, keepdims=True))
    counts = jnp.broadcast_to(counts, (row_total // group_size, group_size, active.shape[1])).reshape(active.shape)
    divisor = counts + 1.0 - active
    return jnp.where(active[:, :, None, None] > 0, summed / divisor[:, :, None, None], stacked)

def reference(features, values, out_grad, query_weight, key_weight, query_mean, query_square, key_mean, key_square, members):

    def flatten(array):
        return array.reshape((N_ROW * N_COL,) + array.shape[2:])
    inputs = (features, values, out_grad, query_weight, key_weight, query_mean, query_square, key_mean, key_square)
    new_query, new_key = lax.map(replica_step, tuple((flatten(array) for array in inputs)))
    new_query = new_query.reshape(query_weight.shape)
    new_key = new_key.reshape(key_weight.shape)
    active_row = members[:, :, 0].astype(jnp.float32)
    active_col = members[:, :, 1].astype(jnp.float32)
    query_row = group_mean(new_query, active_row, GROUP_ROW)
    key_row = group_mean(new_key, active_row, GROUP_ROW)
    query_result = jnp.swapaxes(group_mean(jnp.swapaxes(query_row, 0, 1), jnp.transpose(active_col), GROUP_COL), 0, 1)
    key_result = jnp.swapaxes(group_mean(jnp.swapaxes(key_row, 0, 1), jnp.transpose(active_col), GROUP_COL), 0, 1)
    return (query_result, key_result)
```

```python
import functools
import math
import jax
import jax.numpy as jnp
from jax import lax
from jax.experimental import pallas as pl
from jax.experimental.pallas import tpu as pltpu
from jax.sharding import PartitionSpec as P

HD = 64
SEQ = 512
beta_one = 0.9
beta_two = 0.999
epsilon = 1e-06
decay_rate = 0.01
learn_rate = 0.1
correction_one = 1.0 - math.exp(100.0 * math.log(0.9))
correction_two = 1.0 - math.exp(100.0 * math.log(0.999))
QUAD = 256
PAIR = 128
bf16 = jnp.bfloat16
f32 = jnp.float32

def dot(a, b, ca=1, cb=0):
    return lax.dot_general(a, b, (((ca,), (cb,)), ((), ())), preferred_element_type=f32)

def lamb_direction(w, m, s, g):
    first = beta_one * m + (1.0 - beta_one) * g
    second = beta_two * s + (1.0 - beta_two) * g * g
    return first / correction_one / (jnp.sqrt(second / correction_two) + epsilon) + decay_rate * w

def step_kernel(f_ref, v_ref, og_ref, wq_ref, wk_ref, mq_ref, sq_ref, mk_ref, sk_ref,
                nq_ref, nk_ref, ft, qs, ks, kt, gqt, gks, u_all, norms, *, qb):
    step = pl.program_id(0)
    last = pl.num_programs(0) - 1
    tokens, width = f_ref.shape
    in_scale = 1.0 / math.sqrt(width)
    soft_scale = math.log2(math.e) / math.sqrt(HD)

    @pl.when(step == 0)
    def _():
        ft[...] = f_ref[...].T
        for i in range(4):
            norms[i] = 0.0

    feats = f_ref[...]
    qs[...] = (dot(feats, wq_ref[...].astype(bf16)) * in_scale).astype(bf16)
    keys = (dot(feats, wk_ref[...].astype(bf16)) * in_scale).astype(bf16)
    ks[...] = keys
    kt[...] = keys.T
    lane = lax.broadcasted_iota(jnp.int32, (1, PAIR), 1)
    for s in range(tokens // SEQ):
        rows = slice(s * SEQ, (s + 1) * SEQ)
        for p in range(QUAD // PAIR):
            lanes = slice(p * PAIR, (p + 1) * PAIR)
            k_pair = ks[rows, lanes]
            v_pair = v_ref[rows, lanes]
            gk = jnp.zeros((SEQ, PAIR), f32)
            for h in range(PAIR // HD):
                keep = (lane >= h * HD) & (lane < (h + 1) * HD)
                head = p * PAIR + h * HD
                for b in range(SEQ // qb):
                    at = slice(s * SEQ + b * qb, s * SEQ + (b + 1) * qb)
                    q_head = jnp.where(keep, qs[at, lanes], jnp.zeros((), bf16))
                    o_head = jnp.where(keep, og_ref[at, lanes] * (1.0 / math.sqrt(HD)), 0.0).astype(bf16)
                    st = dot(k_pair, q_head, 1, 1)
                    gp = dot(v_pair, o_head, 1, 1)
                    top = jnp.max(st, axis=0, keepdims=True)
                    e = jnp.exp2((st - top) * soft_scale)
                    inv = 1.0 / jnp.sum(e, axis=0, keepdims=True)
                    prob = e * inv
                    low = prob.astype(bf16).astype(f32)
                    delta = jnp.sum(low * gp, axis=0, keepdims=True)
                    ds = (prob * (gp - delta)).astype(bf16)
                    gk = gk + dot(ds, q_head)
                    gqt[head:head + HD, at] = dot(kt[head:head + HD, rows], ds).astype(bf16)
            gks[rows, lanes] = gk.astype(bf16)
    gq = dot(ft[...], gqt[...], 1, 1) * in_scale
    gk = dot(ft[...], gks[...]) * in_scale
    wq = wq_ref[...]
    wk = wk_ref[...]
    uq = lamb_direction(wq, mq_ref[...], sq_ref[...], gq)
    uk = lamb_direction(wk, mk_ref[...], sk_ref[...], gk)
    cols = pl.ds(pl.multiple_of(step * QUAD, QUAD), QUAD)
    u_all[0, :, cols] = uq
    u_all[1, :, cols] = uk
    nq_ref[:, cols] = wq
    nk_ref[:, cols] = wk
    norms[0] += jnp.sum(wq * wq)
    norms[1] += jnp.sum(uq * uq)
    norms[2] += jnp.sum(wk * wk)
    norms[3] += jnp.sum(uk * uk)

    @pl.when(step == last)
    def _():
        def ratio(i):
            w2 = jnp.full((1, 1), norms[i], f32)
            u2 = jnp.full((1, 1), norms[i + 1], f32)
            return learn_rate * jnp.sqrt(w2) / jnp.sqrt(u2 + epsilon)
        nq_ref[...] = nq_ref[...] - ratio(0) * u_all[0]
        nk_ref[...] = nk_ref[...] - ratio(2) * u_all[1]

def local_step(f, v, og, wq, wk, mq, sq, mk, sk, qb=512):
    tokens, width = f.shape
    heads = wq.shape[1]
    full = pl.BlockSpec((tokens, width), lambda i: (0, 0))
    tok = pl.BlockSpec((tokens, QUAD), lambda i: (0, i))
    wsp = pl.BlockSpec((width, QUAD), lambda i: (0, i))
    osp = pl.BlockSpec((width, heads), lambda i: (0, 0))
    return pl.pallas_call(
        functools.partial(step_kernel, qb=qb),
        grid=(heads // QUAD,),
        in_specs=[full, tok, tok] + [wsp] * 6,
        out_specs=[osp, osp],
        out_shape=[jax.ShapeDtypeStruct((width, heads), f32)] * 2,
        scratch_shapes=[
            pltpu.VMEM((width, tokens), bf16),
            pltpu.VMEM((tokens, QUAD), bf16),
            pltpu.VMEM((tokens, QUAD), bf16),
            pltpu.VMEM((QUAD, tokens), bf16),
            pltpu.VMEM((QUAD, tokens), bf16),
            pltpu.VMEM((tokens, QUAD), bf16),
            pltpu.VMEM((2, width, heads), f32),
            pltpu.SMEM((4,), f32),
        ],
        compiler_params=pltpu.CompilerParams(vmem_limit_bytes=56 << 20),
    )(f, v, og, wq, wk, mq, sq, mk, sk)


CHUNKS = 2
GROUP = 4


def ring(axis, step):
    size = lax.axis_size(axis)
    return [(i, i - i % GROUP + (i + step) % GROUP) for i in range(size)]


def swap(axis, bit):
    return [(i, i ^ bit) for i in range(lax.axis_size(axis))]


def member_facts(members):
    r = lax.axis_index("row")
    c = lax.axis_index("col")
    grid = lax.all_gather(members, ("row", "col"))
    grid = grid.reshape(lax.axis_size("row"), lax.axis_size("col"), 2)
    base_r = r - r % GROUP
    base_c = c - c % GROUP
    here = lax.dynamic_slice_in_dim(grid, c, 1, axis=1)[:, 0, 0]
    column = lax.dynamic_slice_in_dim(here, base_r, GROUP)
    count_a = jnp.sum(column)
    pair = lax.dynamic_slice_in_dim(grid, r - r % 2, 2, axis=0)
    pair = jnp.where(r % 2 == 0, pair, pair[::-1])
    own = lax.dynamic_slice_in_dim(pair, c, 1, axis=1)[:, 0]
    count_b = jnp.sum(lax.dynamic_slice_in_dim(pair[:, :, 1], base_c, GROUP, axis=1), axis=1)
    return own[:, 0], own[:, 1], jnp.maximum(count_a, 1.0), jnp.maximum(count_b, 1.0)


def average(full, facts, at, rows):
    in_a, in_b, count_a, count_b = facts
    core = lax.axis_index("row") % 2
    y = lax.axis_index("col") % GROUP
    half = full.shape[0] // 2
    width = full.shape[1]
    mine = lax.dynamic_slice_in_dim(full, core * half + at, rows)
    other = lax.dynamic_slice_in_dim(full, (1 - core) * half + at, rows)
    theirs = lax.ppermute(other, "row", swap("row", 1))
    part = in_a[0] * mine + in_a[1] * theirs
    far = lax.ppermute(part, "row", swap("row", 2))
    mean = (part + far) / count_a
    held = jnp.stack([jnp.where(in_a[0] > 0, mean, mine), jnp.where(in_a[1] > 0, mean, theirs)])
    piece = rows // GROUP
    cut = piece // 2

    def block(d):
        got = lax.dynamic_slice_in_dim(held, (y + d) % GROUP * piece, piece, axis=1)
        return got * in_b[:, None, None]

    opposite = block(2)
    fwd = lax.ppermute(opposite[:, :cut], "col", ring("col", 1))
    bwd = lax.ppermute(opposite[:, cut:], "col", ring("col", -1))
    none = jnp.zeros_like(fwd)
    to_next = block(1) + jnp.concatenate([fwd, none], axis=1)
    to_prev = block(3) + jnp.concatenate([none, bwd], axis=1)
    from_prev = lax.ppermute(to_next, "col", ring("col", 1))
    from_next = lax.ppermute(to_prev, "col", ring("col", -1))
    total = (block(0) + from_prev + from_next) / count_b[:, None, None]
    before = lax.ppermute(total, "col", ring("col", 1))
    after = lax.ppermute(total, "col", ring("col", -1))
    low = lax.ppermute(before[:, :cut], "col", ring("col", 1))
    high = lax.ppermute(after[:, cut:], "col", ring("col", -1))
    cycle = jnp.concatenate([total, after, low, high, before] * 2, axis=1)
    means = lax.dynamic_slice_in_dim(cycle, (GROUP - y) % GROUP * piece, rows, axis=1)
    final = jnp.where(in_b[:, None, None] > 0, means, held)
    mate = lax.ppermute(final[1], "row", swap("row", 1))
    return final[0], mate


def per_device(
    features,
    values,
    out_grad,
    query_weight,
    key_weight,
    query_mean,
    query_square,
    key_mean,
    key_square,
    members,
):
    facts = member_facts(members[0, 0].astype(f32))
    new = local_step(
        features[0, 0],
        values[0, 0],
        out_grad[0, 0],
        query_weight[0, 0],
        key_weight[0, 0],
        query_mean[0, 0],
        query_square[0, 0],
        key_mean[0, 0],
        key_square[0, 0],
    )
    core = lax.axis_index("row") % 2
    outs = []
    per_matrix = CHUNKS // 2
    for full in new:
        rows = full.shape[0] // 2 // per_matrix
        parts = [average(full, facts, j * rows, rows) for j in range(per_matrix)]
        own = jnp.concatenate([p[0] for p in parts])
        mate = jnp.concatenate([p[1] for p in parts])
        first = jnp.where(core == 0, own, mate)
        second = jnp.where(core == 0, mate, own)
        outs.append(jnp.concatenate([first, second])[None, None])
    return tuple(outs)


def solution(mesh):
    mats = P("row", "col", None, None)
    return jax.shard_map(
        per_device,
        mesh=mesh,
        in_specs=(mats,) * 9 + (P("row", "col", None),),
        out_specs=(mats, mats),
        check_vma=False,
    )
```

```python
import functools
import math

import jax
import jax.numpy as jnp
from jax import lax
from jax.experimental import pallas as pl
from jax.experimental.pallas import tpu as pltpu
from jax.sharding import PartitionSpec as P

HD = 64
SEQ = 512
QUAD = 256
PAIR = 128
GROUP = 4
NOTE = 8
CHUNKS = ((64, 0), (0, 64))
bf16 = jnp.bfloat16
f32 = jnp.float32

beta_one = 0.9
beta_two = 0.999
epsilon = 1e-06
decay_rate = 0.01
learn_rate = 0.1
correction_one = 1.0 - math.exp(100.0 * math.log(0.9))
correction_two = 1.0 - math.exp(100.0 * math.log(0.999))


def dot(a, b, ca=1, cb=0):
    return lax.dot_general(a, b, (((ca,), (cb,)), ((), ())), preferred_element_type=f32)


def lamb_direction(w, m, s, g):
    first = beta_one * m + (1.0 - beta_one) * g
    second = beta_two * s + (1.0 - beta_two) * g * g
    return first / correction_one / (jnp.sqrt(second / correction_two) + epsilon) + decay_rate * w


def lamb_ratio(norms):
    w2 = jnp.full((1, 1), norms[0], f32)
    u2 = jnp.full((1, 1), norms[1], f32)
    return learn_rate * jnp.sqrt(w2) / jnp.sqrt(u2 + epsilon)


def only_head(pair, h):
    lane = lax.broadcasted_iota(jnp.int32, (1, PAIR), 1)
    return jnp.where((lane >= h * HD) & (lane < (h + 1) * HD), pair, jnp.zeros((), pair.dtype))


def core_at():
    return lax.axis_index("row") % 2


def ring_at():
    return lax.axis_index("col") % GROUP


def deal(core, fill, mine, other, mat, size):
    for side, outs in ((core, mine), (1 - core, other)):
        at = side * (size // 2)
        for chunk, out in zip(CHUNKS, outs):
            count = chunk[mat]
            skip = chunk[0] if mat else 0
            if not count:
                continue
            for j in range(GROUP):
                to = j * sum(chunk) + skip
                out[to : to + count] = fill(pl.ds(pl.multiple_of(at, 8), count))
                at = at + count


def query_kernel(
    members, f_ref, v_ref, o_ref, wq_ref, wk_ref, m_ref, s_ref,
    mine0, other0, mine1, other1, facts_ref, ds_ref, q_ref, ft_ref, ks, kt, gqt, u_all, w_all, norms,
):
    step = pl.program_id(0)
    last = pl.num_programs(0) - 1
    tokens, width = f_ref.shape
    in_scale = 1.0 / math.sqrt(width)
    soft_scale = math.log2(math.e) / math.sqrt(HD)
    cols = pl.ds(pl.multiple_of(step * QUAD, QUAD), QUAD)

    @pl.when(step == 0)
    def _():
        ft_ref[...] = f_ref[...].T
        norms[0] = 0.0
        norms[1] = 0.0

    feats = f_ref[...]
    queries = (dot(feats, wq_ref[...].astype(bf16)) * in_scale).astype(bf16)
    q_ref[:, cols] = queries
    keys = (dot(feats, wk_ref[...].astype(bf16)) * in_scale).astype(bf16)
    ks[...] = keys
    kt[...] = keys.T
    for s in range(tokens // SEQ):
        rows = slice(s * SEQ, (s + 1) * SEQ)
        for p in range(QUAD // PAIR):
            lanes = slice(p * PAIR, (p + 1) * PAIR)
            for h in range(PAIR // HD):
                head = p * PAIR + h * HD
                o_head = only_head(o_ref[rows, lanes], h) * (1.0 / math.sqrt(HD))
                scores = dot(ks[rows, lanes], only_head(queries[rows, lanes], h), 1, 1)
                grad_prob = dot(v_ref[rows, lanes], o_head.astype(bf16), 1, 1)
                top = jnp.max(scores, axis=0, keepdims=True)
                e = jnp.exp2((scores - top) * soft_scale)
                prob = e * (1.0 / jnp.sum(e, axis=0, keepdims=True))
                prob_low = prob.astype(bf16).astype(f32)
                delta = jnp.sum(prob_low * grad_prob, axis=0, keepdims=True)
                grad_score = (prob * (grad_prob - delta)).astype(bf16)
                unit = step * (QUAD // HD) + head // HD
                ds_ref[unit, rows, :] = grad_score
                gqt[head : head + HD, rows] = dot(kt[head : head + HD, rows], grad_score).astype(bf16)
    grad = dot(ft_ref[...], gqt[...], 1, 1) * in_scale
    w = wq_ref[...]
    u = lamb_direction(w, m_ref[...], s_ref[...], grad)
    u_all[:, cols] = u
    w_all[:, cols] = w
    norms[0] += jnp.sum(w * w)
    norms[1] += jnp.sum(u * u)

    @pl.when(step == last)
    def _():
        ratio = lamb_ratio(norms)
        new = lambda here: w_all[here, :] - ratio * u_all[here, :]
        deal(core_at(), new, (mine0, mine1), (other0, other1), 0, width)
        at = lax.broadcasted_iota(jnp.int32, facts_ref.shape, 0)
        facts = jnp.where(at == 0, members[0], jnp.where(at == 1, members[1], 0)).astype(f32)
        facts_ref[...] = facts
        other0[mine0.shape[0] :] = facts


def key_kernel(
    ds_ref, q_ref, ft_ref, query_mine, query_other, w_ref, m_ref, s_ref,
    mine1, other1, gks, u_all, w_all, norms,
):
    step = pl.program_id(0)
    last = pl.num_programs(0) - 1
    tokens, width = q_ref.shape
    in_scale = 1.0 / math.sqrt(width)
    cols = pl.ds(pl.multiple_of(step * QUAD, QUAD), QUAD)

    @pl.when(step == 0)
    def _():
        norms[0] = 0.0
        norms[1] = 0.0

    for s in range(tokens // SEQ):
        rows = slice(s * SEQ, (s + 1) * SEQ)
        for p in range(QUAD // PAIR):
            lanes = pl.ds(pl.multiple_of(step * QUAD + p * PAIR, PAIR), PAIR)
            pair = q_ref[rows, lanes]
            grad = jnp.zeros((SEQ, PAIR), f32)
            for h in range(PAIR // HD):
                unit = step * (QUAD // HD) + p * (PAIR // HD) + h
                grad = grad + dot(ds_ref[unit, rows, :], only_head(pair, h))
            gks[rows, p * PAIR : (p + 1) * PAIR] = grad.astype(bf16)
    grad = dot(ft_ref[...], gks[...]) * in_scale
    w = w_ref[...]
    u = lamb_direction(w, m_ref[...], s_ref[...], grad)
    u_all[:, cols] = u
    w_all[:, cols] = w
    norms[0] += jnp.sum(w * w)
    norms[1] += jnp.sum(u * u)

    @pl.when(step == last)
    def _():
        ratio = lamb_ratio(norms)
        new = lambda here: w_all[here, :] - ratio * u_all[here, :]
        deal(core_at(), new, (None, mine1), (None, other1), 1, width)
        for j in range(GROUP):
            here = slice(j * sum(CHUNKS[1]), j * sum(CHUNKS[1]) + CHUNKS[1][0])
            if CHUNKS[1][0]:
                mine1[here] = query_mine[here]
                other1[here] = query_other[here]


SCALARS = pl.BlockSpec(memory_space=pltpu.SMEM)
STAYS = pl.BlockSpec(memory_space=pltpu.VMEM)


def in_hbm(*xs):
    return [pltpu.with_memory_space_constraint(x, pltpu.HBM) for x in xs]


def in_vmem(*xs):
    return [pltpu.with_memory_space_constraint(x, pltpu.VMEM) for x in xs]


def chunk_rows(c):
    return GROUP * sum(CHUNKS[c])


def query_step(members, f, v, o, wq, wk, m, s):
    tokens, width = f.shape
    heads = wq.shape[1]
    tok = pl.BlockSpec((tokens, QUAD), lambda i: (0, i))
    mat = pl.BlockSpec((width, QUAD), lambda i: (0, i))
    full = pl.BlockSpec((tokens, width), lambda i: (0, 0))
    later = chunk_rows(1) if CHUNKS[1][0] else NOTE
    shapes = [(chunk_rows(0), heads), (chunk_rows(0) + NOTE, heads), (later, heads), (later, heads), (NOTE, heads)]
    return pl.pallas_call(
        query_kernel,
        grid=(heads // QUAD,),
        in_specs=[SCALARS, full, tok, tok, mat, mat, mat, mat],
        out_specs=[STAYS] * 8,
        out_shape=[pltpu.VMEM(x, f32) for x in shapes]
        + [pltpu.VMEM(x, bf16) for x in ((heads // HD, tokens, SEQ), (tokens, heads), (width, tokens))],
        scratch_shapes=[
            pltpu.VMEM((tokens, QUAD), bf16),
            pltpu.VMEM((QUAD, tokens), bf16),
            pltpu.VMEM((QUAD, tokens), bf16),
            pltpu.VMEM((width, heads), f32),
            pltpu.VMEM((width, heads), f32),
            pltpu.SMEM((2,), f32),
        ],
        compiler_params=pltpu.CompilerParams(vmem_limit_bytes=36 << 20),
        name="query_step",
    )(members, *in_hbm(f, v, o, wq, wk, m, s))


def key_step(ds, q, ft, query_mine, query_other, w, m, s):
    tokens, heads = q.shape
    width = ft.shape[0]
    mat = pl.BlockSpec((width, QUAD), lambda i: (0, i))
    return pl.pallas_call(
        key_kernel,
        grid=(heads // QUAD,),
        in_specs=[STAYS] * 5 + [mat, mat, mat],
        out_specs=[STAYS] * 2,
        out_shape=[pltpu.VMEM((chunk_rows(1), heads), f32)] * 2,
        scratch_shapes=[
            pltpu.VMEM((tokens, QUAD), bf16),
            pltpu.VMEM((width, heads), f32),
            pltpu.VMEM((width, heads), f32),
            pltpu.SMEM((2,), f32),
        ],
        compiler_params=pltpu.CompilerParams(vmem_limit_bytes=24 << 20),
        name="key_step",
    )(*in_vmem(ds, q, ft, query_mine, query_other), *in_hbm(w, m, s))


A_ME, B_ME, A_MATE, B_MATE, A_CHIP, A_COUNT, B_COUNT, B_COUNT_MATE = range(8)
DISTANCES = (1, 3, 2)
NO_HBM = pl.CostEstimate(flops=0, transcendentals=0, bytes_accessed=0)


def small_call(kernel, name, shapes, *operands):
    got = pl.pallas_call(
        kernel,
        in_specs=[STAYS] * len(operands),
        out_specs=[STAYS] * len(shapes),
        out_shape=[pltpu.VMEM(s, f32) for s in shapes],
        compiler_params=pltpu.CompilerParams(vmem_limit_bytes=8 << 20),
        cost_estimate=NO_HBM,
        name=name,
    )(*in_vmem(*operands))
    return list(got)


def row(facts, i):
    return facts[i : i + 1, :]


def chip_sum(mine, theirs, facts, first):
    rows, width = mine.shape

    def kernel(mine_ref, theirs_ref, facts_ref, out_ref, *maybe_facts):
        f = facts_ref[...]
        if first:
            got = theirs_ref[rows:]
            at = lax.broadcasted_iota(jnp.int32, f.shape, 0)
            f = jnp.where(at == A_MATE, row(got, 0), jnp.where(at == B_MATE, row(got, 1), f))
            f = jnp.where(at == A_CHIP, row(f, A_ME) + row(f, A_MATE), f)
            out_ref[rows:] = f
            maybe_facts[0][...] = f
        out_ref[:rows] = row(f, A_ME) * mine_ref[...] + row(f, A_MATE) * theirs_ref[:rows]

    shapes = [(rows + NOTE, width), facts.shape] if first else [(rows, width)]
    got = small_call(kernel, "chip_sum", shapes, mine, theirs, facts)
    return got if first else got + [facts]


def row_mean(mine, theirs, far, facts, first):
    rows, width = mine.shape
    piece = rows // GROUP

    def kernel(mine_ref, theirs_ref, far_ref, facts_ref, own, s1, s2, s3, held, held_mate, *maybe_facts):
        f = facts_ref[...]
        if first:
            at = lax.broadcasted_iota(jnp.int32, f.shape, 0)
            count = row(f, A_CHIP) + row(far_ref[rows:], A_CHIP)
            f = jnp.where(at == A_COUNT, jnp.maximum(count, 1.0), f)
            maybe_facts[0][...] = f
        y = ring_at()
        for d, out in enumerate((own, s1, s2, s3)):
            here = pl.ds(pl.multiple_of((y + d) % GROUP * piece, 8), piece)
            m, t = mine_ref[here, :], theirs_ref[here, :]
            mean = (row(f, A_ME) * m + row(f, A_MATE) * t + far_ref[here, :]) / row(f, A_COUNT)
            m = jnp.where(row(f, A_ME) > 0, mean, m)
            t = jnp.where(row(f, A_MATE) > 0, mean, t)
            held[here, :] = m
            held_mate[here, :] = t
            out[:piece] = m * row(f, B_ME)
            out[piece : 2 * piece] = t * row(f, B_MATE)
            if first and d:
                out[2 * piece :] = f

    sent = (2 * piece + (NOTE if first else 0), width)
    shapes = [(2 * piece, width), sent, sent, sent, (rows, width), (rows, width)]
    if first:
        shapes = shapes + [facts.shape]
    got = small_call(kernel, "row_mean", shapes, mine, theirs, far, facts)
    return got if first else got + [facts]


def col_mean(own, got, facts, first):
    rows, width = own.shape
    piece = rows // 2

    def kernel(own_ref, g1, g2, g3, facts_ref, me, mate, *maybe_facts):
        f = facts_ref[...]
        if first:
            at = lax.broadcasted_iota(jnp.int32, f.shape, 0)
            notes = [g[rows:] for g in (g1, g2, g3)]
            count = sum([row(n, B_ME) for n in notes], row(f, B_ME))
            count_mate = sum([row(n, B_MATE) for n in notes], row(f, B_MATE))
            f = jnp.where(at == B_COUNT, jnp.maximum(count, 1.0), f)
            f = jnp.where(at == B_COUNT_MATE, jnp.maximum(count_mate, 1.0), f)
            maybe_facts[0][...] = f
        total = own_ref[...] + g1[:rows] + g2[:rows] + g3[:rows]
        me[...] = total[:piece] / row(f, B_COUNT)
        mate[...] = total[piece:] / row(f, B_COUNT_MATE)

    shapes = [(piece, width), (piece, width)] + ([facts.shape] if first else [])
    got = small_call(kernel, "col_mean", shapes, own, *got, facts)
    return got if first else got + [facts]


def joined(me, mate):
    piece, width = me.shape

    def kernel(me_ref, mate_ref, out):
        out[:piece] = me_ref[...]
        out[piece:] = mate_ref[...]

    return small_call(kernel, "joined", [(2 * piece, width)], me, mate)[0]


def finish(mat, size, parts, facts):
    width = facts.shape[1]
    half = size // 2

    def kernel(*refs):
        facts_ref, out_ref, made, sems = refs[-4:]
        takes = row(facts_ref[...], B_ME) > 0
        core, y = core_at(), ring_at()
        copies = []
        base = sum(GROUP * CHUNKS[c][mat] for c in range(parts[0][0]))
        for n, (c, *_) in enumerate(parts):
            count, piece = CHUNKS[c][mat], sum(CHUNKS[c])
            skip = CHUNKS[c][0] if mat else 0
            held, held_mate, *pieces = refs[6 * n : 6 * n + 6]
            for side, (whose, kept) in enumerate(((core, held), (1 - core, held_mate))):
                for d, src in enumerate(pieces):
                    j = (y + GROUP - d) % GROUP
                    old = kept[pl.ds(pl.multiple_of(j * piece + skip, 8), count), :]
                    here = pl.ds(pl.multiple_of(whose * half + base + j * count, 8), count)
                    made[here, :] = jnp.where(takes, src[side * piece + skip : side * piece + skip + count], old)
                    copy = pltpu.make_async_copy(made.at[here, :], out_ref.at[here, :], sems.at[len(copies)])
                    copy.start()
                    copies.append(copy)
            base += GROUP * count
        for copy in copies:
            copy.wait()

    operands = [x for _, held, held_mate, pieces in parts for x in (held, held_mate, *pieces)]
    return pl.pallas_call(
        kernel,
        in_specs=[STAYS] * (len(operands) + 1),
        out_specs=pl.BlockSpec(memory_space=pl.ANY),
        out_shape=jax.ShapeDtypeStruct((size, width), f32),
        scratch_shapes=[pltpu.VMEM((size, width), f32), pltpu.SemaphoreType.DMA((2 * GROUP * len(parts),))],
        compiler_params=pltpu.CompilerParams(vmem_limit_bytes=8 << 20),
        name="finish",
    )(*in_vmem(*operands, facts))


def ring(step):
    size = lax.axis_size("col")
    return [(i, i - i % GROUP + (i + step) % GROUP) for i in range(size)]


def swap(bit):
    return [(i, i ^ bit) for i in range(lax.axis_size("row"))]


def to_mate(x):
    return lax.ppermute(x, "row", swap(1))


def to_far(x):
    return lax.ppermute(x, "row", swap(2))


def around(xs):
    got = {d: lax.ppermute(xs[d - 1], "col", ring(d)) for d in DISTANCES}
    return [got[d] for d in (1, 2, 3)]


def tie(*xs):
    return lax.optimization_barrier(xs)


def per_device(features, values, out_grad, query_weight, key_weight, query_mean, query_square, key_mean, key_square, members):
    f, v, o, wq, wk = [a[0, 0] for a in (features, values, out_grad, query_weight, key_weight)]
    mq, sq, mk, sk = [a[0, 0] for a in (query_mean, query_square, key_mean, key_square)]
    size = wq.shape[0]

    mine0, other0, query_mine, query_other, facts, ds, queries, ft = query_step(members[0, 0], f, v, o, wq, wk, mq, sq)
    theirs0 = to_mate(other0)
    part0, facts = chip_sum(mine0, theirs0, facts, True)
    part0, ds = tie(part0, ds)
    far0 = to_far(part0)
    mine1, other1 = key_step(ds, queries, ft, query_mine, query_other, wk, mk, sk)
    theirs1 = to_mate(other1)
    part1, _ = chip_sum(mine1, theirs1, facts, False)
    far0, part1 = tie(far0, part1)
    far1 = to_far(part1)

    def total_of(own, got, facts, first):
        me, mate, facts = col_mean(own, got, facts, first)
        return joined(me, to_mate(mate)), facts

    def gather(total):
        return [total] + around([total] * 3)

    own0, *send0, held0, held_mate0, facts = row_mean(mine0, theirs0, far0, facts, True)
    total0, facts = total_of(own0, around(send0), facts, True)
    held_mate0 = to_mate(held_mate0)
    far1, _ = tie(far1, total0)
    all0 = gather(total0)
    own1, *send1, held1, held_mate1, _ = row_mean(mine1, theirs1, far1, facts, False)
    got1 = around(send1)
    own1, *all0 = tie(own1, *all0)
    total1, _ = total_of(own1, got1, facts, False)
    held_mate1 = to_mate(held_mate1)
    all1 = gather(total1)
    zero, one = (0, held0, held_mate0, all0), (1, held1, held_mate1, all1)
    if CHUNKS[1][0]:
        query = finish(0, size, [zero, one], facts)
    else:
        query = finish(0, size, [zero], facts)
        all1[1], query = tie(all1[1], query)
    key = finish(1, size, [one], facts)
    return query[None, None], key[None, None]


def solution(mesh):
    mats = P("row", "col", None, None)
    return jax.shard_map(
        per_device,
        mesh=mesh,
        in_specs=(mats,) * 9 + (P("row", "col", None),),
        out_specs=(mats, mats),
        check_vma=False,
    )
```

```python
import functools
import math

import jax
import jax.numpy as jnp
from jax import lax
from jax.experimental import pallas as pl
from jax.experimental.pallas import tpu as pltpu
from jax.sharding import PartitionSpec as P

HD = 64
SEQ = 512
QUAD = 256
PAIR = 128
GROUP = 4
NOTE = 8
bf16 = jnp.bfloat16
f32 = jnp.float32

beta_one = 0.9
beta_two = 0.999
epsilon = 1e-06
decay_rate = 0.01
learn_rate = 0.1
correction_one = 1.0 - math.exp(100.0 * math.log(0.9))
correction_two = 1.0 - math.exp(100.0 * math.log(0.999))


def dot(a, b, ca=1, cb=0):
    return lax.dot_general(a, b, (((ca,), (cb,)), ((), ())), preferred_element_type=f32)


def lamb_direction(w, m, s, g):
    first = beta_one * m + (1.0 - beta_one) * g
    second = beta_two * s + (1.0 - beta_two) * g * g
    return first / correction_one / (jnp.sqrt(second / correction_two) + epsilon) + decay_rate * w


def lamb_ratio(norms):
    w2 = jnp.full((1, 1), norms[0], f32)
    u2 = jnp.full((1, 1), norms[1], f32)
    return learn_rate * jnp.sqrt(w2) / jnp.sqrt(u2 + epsilon)


def only_head(pair, h):
    lane = lax.broadcasted_iota(jnp.int32, (1, PAIR), 1)
    return jnp.where((lane >= h * HD) & (lane < (h + 1) * HD), pair, jnp.zeros((), pair.dtype))


def core_at():
    return lax.axis_index("row") % 2


def ring_at():
    return lax.axis_index("col") % GROUP


def deal(fill, size, mine, other):
    half = size // 2
    for side, out in ((core_at(), mine), (1 - core_at(), other)):
        out[:half] = fill(pl.ds(pl.multiple_of(side * half, 8), half))


def query_kernel(
    members, f_ref, v_ref, o_ref, wq_ref, wk_ref, m_ref, s_ref,
    mine_ref, other_ref, facts_ref, ds_ref, q_ref, ft_ref, ks, kt, gqt, u_all, w_all, norms,
):
    step = pl.program_id(0)
    last = pl.num_programs(0) - 1
    tokens, width = f_ref.shape
    in_scale = 1.0 / math.sqrt(width)
    soft_scale = math.log2(math.e) / math.sqrt(HD)
    cols = pl.ds(pl.multiple_of(step * QUAD, QUAD), QUAD)

    @pl.when(step == 0)
    def _():
        ft_ref[...] = f_ref[...].T
        norms[0] = 0.0
        norms[1] = 0.0

    feats = f_ref[...]
    queries = (dot(feats, wq_ref[...].astype(bf16)) * in_scale).astype(bf16)
    q_ref[:, cols] = queries
    keys = (dot(feats, wk_ref[...].astype(bf16)) * in_scale).astype(bf16)
    ks[...] = keys
    kt[...] = keys.T
    units = [(s, head) for s in range(tokens // SEQ) for head in range(0, QUAD, HD)]

    def products(s, head):
        rows = slice(s * SEQ, (s + 1) * SEQ)
        lanes = slice(head // PAIR * PAIR, head // PAIR * PAIR + PAIR)
        h = head % PAIR // HD
        o_head = only_head(o_ref[rows, lanes], h) * (1.0 / math.sqrt(HD))
        scores = dot(ks[rows, lanes], only_head(queries[rows, lanes], h), 1, 1)
        return scores, dot(v_ref[rows, lanes], o_head.astype(bf16), 1, 1)

    ready = products(*units[0])
    for i, (s, head) in enumerate(units):
        rows = slice(s * SEQ, (s + 1) * SEQ)
        scores, grad_prob = ready
        if i + 1 < len(units):
            ready = products(*units[i + 1])
        top = jnp.max(scores, axis=0, keepdims=True)
        e = jnp.exp2((scores - top) * soft_scale)
        prob = e * (1.0 / jnp.sum(e, axis=0, keepdims=True))
        prob_low = prob.astype(bf16).astype(f32)
        delta = jnp.sum(prob_low * grad_prob, axis=0, keepdims=True)
        grad_score = (prob * (grad_prob - delta)).astype(bf16)
        ds_ref[step * (QUAD // HD) + head // HD, rows, :] = grad_score
        gqt[head : head + HD, rows] = dot(kt[head : head + HD, rows], grad_score).astype(bf16)
    grad = dot(ft_ref[...], gqt[...], 1, 1) * in_scale
    w = wq_ref[...]
    u = lamb_direction(w, m_ref[...], s_ref[...], grad)
    u_all[:, cols] = u
    w_all[:, cols] = w
    norms[0] += jnp.sum(w * w)
    norms[1] += jnp.sum(u * u)

    @pl.when(step == last)
    def _():
        ratio = lamb_ratio(norms)
        new = lambda here: w_all[here, :] - ratio * u_all[here, :]
        deal(new, width, mine_ref, other_ref)
        at = lax.broadcasted_iota(jnp.int32, facts_ref.shape, 0)
        facts = jnp.where(at == 0, members[0, 0, 0], jnp.where(at == 1, members[0, 0, 1], 0)).astype(f32)
        facts_ref[...] = facts
        other_ref[width // 2 :] = facts


def key_kernel(
    ds_ref, q_ref, ft_ref, w_ref, m_ref, s_ref,
    mine_ref, other_ref, gks, u_all, w_all, norms,
):
    step = pl.program_id(0)
    last = pl.num_programs(0) - 1
    tokens, width = q_ref.shape
    in_scale = 1.0 / math.sqrt(width)
    cols = pl.ds(pl.multiple_of(step * QUAD, QUAD), QUAD)

    @pl.when(step == 0)
    def _():
        norms[0] = 0.0
        norms[1] = 0.0

    for s in range(tokens // SEQ):
        rows = slice(s * SEQ, (s + 1) * SEQ)
        for p in range(QUAD // PAIR):
            lanes = pl.ds(pl.multiple_of(step * QUAD + p * PAIR, PAIR), PAIR)
            pair = q_ref[rows, lanes]
            grad = jnp.zeros((SEQ, PAIR), f32)
            for h in range(PAIR // HD):
                unit = step * (QUAD // HD) + p * (PAIR // HD) + h
                grad = grad + dot(ds_ref[unit, rows, :], only_head(pair, h))
            gks[rows, p * PAIR : (p + 1) * PAIR] = grad.astype(bf16)
    grad = dot(ft_ref[...], gks[...]) * in_scale
    w = w_ref[...]
    u = lamb_direction(w, m_ref[...], s_ref[...], grad)
    u_all[:, cols] = u
    w_all[:, cols] = w
    norms[0] += jnp.sum(w * w)
    norms[1] += jnp.sum(u * u)

    @pl.when(step == last)
    def _():
        ratio = lamb_ratio(norms)
        new = lambda here: w_all[here, :] - ratio * u_all[here, :]
        deal(new, width, mine_ref, other_ref)


SCALARS = pl.BlockSpec(memory_space=pltpu.SMEM)
STAYS = pl.BlockSpec(memory_space=pltpu.VMEM)


def in_hbm(*xs):
    return [pltpu.with_memory_space_constraint(x, pltpu.HBM) for x in xs]


def in_vmem(*xs):
    return [pltpu.with_memory_space_constraint(x, pltpu.VMEM) for x in xs]


def query_step(members, f, v, o, wq, wk, m, s):
    tokens, width = f.shape
    heads = wq.shape[1]
    tok = pl.BlockSpec((tokens, QUAD), lambda i: (0, i))
    mat = pl.BlockSpec((width, QUAD), lambda i: (0, i))
    full = pl.BlockSpec((tokens, width), lambda i: (0, 0))
    shapes = [(width // 2, heads), (width // 2 + NOTE, heads), (NOTE, heads)]
    return pl.pallas_call(
        query_kernel,
        grid=(heads // QUAD,),
        in_specs=[SCALARS, full, tok, tok, mat, mat, mat, mat],
        out_specs=[STAYS] * 6,
        out_shape=[pltpu.VMEM(x, f32) for x in shapes]
        + [pltpu.VMEM(x, bf16) for x in ((heads // HD, tokens, SEQ), (tokens, heads), (width, tokens))],
        scratch_shapes=[
            pltpu.VMEM((tokens, QUAD), bf16),
            pltpu.VMEM((QUAD, tokens), bf16),
            pltpu.VMEM((QUAD, tokens), bf16),
            pltpu.VMEM((width, heads), f32),
            pltpu.VMEM((width, heads), f32),
            pltpu.SMEM((2,), f32),
        ],
        compiler_params=pltpu.CompilerParams(vmem_limit_bytes=36 << 20),
        name="query_step",
    )(*in_hbm(members, f, v, o, wq, wk, m, s))


def key_step(ds, q, ft, w, m, s):
    tokens, heads = q.shape
    width = ft.shape[0]
    mat = pl.BlockSpec((width, QUAD), lambda i: (0, i))
    return pl.pallas_call(
        key_kernel,
        grid=(heads // QUAD,),
        in_specs=[STAYS] * 3 + [mat, mat, mat],
        out_specs=[STAYS] * 2,
        out_shape=[pltpu.VMEM((width // 2, heads), f32)] * 2,
        scratch_shapes=[
            pltpu.VMEM((tokens, QUAD), bf16),
            pltpu.VMEM((width, heads), f32),
            pltpu.VMEM((width, heads), f32),
            pltpu.SMEM((2,), f32),
        ],
        compiler_params=pltpu.CompilerParams(vmem_limit_bytes=24 << 20),
        name="key_step",
    )(*in_vmem(ds, q, ft), *in_hbm(w, m, s))


A_ME, B_ME, A_MATE, B_MATE, A_CHIP, A_COUNT, B_COUNT, B_COUNT_MATE = range(8)
DISTANCES = (2, 1, 3)
NO_HBM = pl.CostEstimate(flops=0, transcendentals=0, bytes_accessed=0)


def small_call(kernel, name, shapes, *operands):
    got = pl.pallas_call(
        kernel,
        in_specs=[STAYS] * len(operands),
        out_specs=[STAYS] * len(shapes),
        out_shape=[pltpu.VMEM(s, f32) for s in shapes],
        compiler_params=pltpu.CompilerParams(vmem_limit_bytes=8 << 20),
        cost_estimate=NO_HBM,
        name=name,
    )(*in_vmem(*operands))
    return list(got)


def row(facts, i):
    return facts[i : i + 1, :]


def chip_sum(mine, theirs, facts, first):
    rows, width = mine.shape

    def kernel(mine_ref, theirs_ref, facts_ref, out_ref, facts_out):
        f = facts_ref[...]
        if first:
            got = theirs_ref[rows:]
            at = lax.broadcasted_iota(jnp.int32, f.shape, 0)
            f = jnp.where(at == A_MATE, row(got, 0), jnp.where(at == B_MATE, row(got, 1), f))
            f = jnp.where(at == A_CHIP, row(f, A_ME) + row(f, A_MATE), f)
        out_ref[rows:] = f
        facts_out[...] = f
        out_ref[:rows] = row(f, A_ME) * mine_ref[...] + row(f, A_MATE) * theirs_ref[:rows]

    return small_call(kernel, "chip_sum", [(rows + NOTE, width), facts.shape], mine, theirs, facts)


def row_mean(mine, theirs, far, facts, first):
    rows, width = mine.shape
    piece = rows // GROUP

    def kernel(mine_ref, theirs_ref, far_ref, facts_ref, own, s2, s1, s3, held, held_mate, *maybe_facts):
        f = facts_ref[...]
        if first:
            at = lax.broadcasted_iota(jnp.int32, f.shape, 0)
            count = row(f, A_CHIP) + row(far_ref[rows:], A_CHIP)
            f = jnp.where(at == A_COUNT, jnp.maximum(count, 1.0), f)
            maybe_facts[0][...] = f
        y = ring_at()
        for d, out in enumerate((own, s1, s2, s3)):
            here = pl.ds(pl.multiple_of((y + d) % GROUP * piece, 8), piece)
            m, t = mine_ref[here, :], theirs_ref[here, :]
            mean = (row(f, A_ME) * m + row(f, A_MATE) * t + far_ref[here, :]) / row(f, A_COUNT)
            m = jnp.where(row(f, A_ME) > 0, mean, m)
            t = jnp.where(row(f, A_MATE) > 0, mean, t)
            held[here, :] = m
            held_mate[here, :] = t
            out[:piece] = m * row(f, B_ME)
            out[piece : 2 * piece] = t * row(f, B_MATE)
            if first and d:
                out[2 * piece :] = f

    sent = (2 * piece + (NOTE if first else 0), width)
    shapes = [(2 * piece, width), sent, sent, sent, (rows, width), (rows, width)]
    if first:
        shapes = shapes + [facts.shape]
    got = small_call(kernel, "row_mean", shapes, mine, theirs, far, facts)
    return got if first else got + [facts]


def col_mean(own, got, facts, first):
    rows, width = own.shape
    piece = rows // 2

    def kernel(own_ref, g1, g2, g3, facts_ref, me, mate):
        f = facts_ref[...]
        if first:
            at = lax.broadcasted_iota(jnp.int32, f.shape, 0)
            notes = [g[rows:] for g in (g1, g2, g3)]
            count = sum([row(n, B_ME) for n in notes], row(f, B_ME))
            count_mate = sum([row(n, B_MATE) for n in notes], row(f, B_MATE))
            f = jnp.where(at == B_COUNT, jnp.maximum(count, 1.0), f)
            f = jnp.where(at == B_COUNT_MATE, jnp.maximum(count_mate, 1.0), f)
            mate[...] = f
        total = own_ref[...] + g1[:rows] + g2[:rows] + g3[:rows]
        me[:piece] = total[:piece] / row(f, B_COUNT)
        mate_out = me.at[piece:] if first else mate
        mate_out[...] = total[piece:] / row(f, B_COUNT_MATE)

    shapes = [(rows, width), facts.shape] if first else [(piece, width), (piece, width)]
    return small_call(kernel, "col_mean", shapes, own, *got, facts)


def joined(me, mate):
    piece, width = me.shape

    def kernel(me_ref, mate_ref, out):
        out[:piece] = me_ref[...]
        out[piece:] = mate_ref[...]

    return small_call(kernel, "joined", [(2 * piece, width)], me, mate)[0]


def choose(held, held_mate, p0, p3, p1, p2, facts):
    rows, width = held.shape
    piece = rows // GROUP

    def kernel(held_ref, held_mate_ref, b0, b3, b1, b2, facts_ref, me, mate):
        f = facts_ref[...]
        for d, src in enumerate((b0, b1, b2, b3)):
            here = pl.ds(pl.multiple_of((ring_at() + GROUP - d) % GROUP * piece, 8), piece)
            me[here, :] = jnp.where(row(f, B_ME) > 0, src[:piece], held_ref[here, :])
            mate[here, :] = jnp.where(row(f, B_MATE) > 0, src[piece:], held_mate_ref[here, :])

    return small_call(kernel, "choose", [(rows, width)] * 2, held, held_mate, p0, p3, p1, p2, facts)


def place(mine, other):
    rows, width = mine.shape

    def kernel(mine_ref, other_ref, out_ref, sems):
        copies = []
        for i, (src, side) in enumerate(((mine_ref, core_at()), (other_ref, 1 - core_at()))):
            to = out_ref.at[pl.ds(pl.multiple_of(side * rows, 8), rows), :]
            copies.append(pltpu.make_async_copy(src, to, sems.at[i]))
            copies[-1].start()
        for copy in copies:
            copy.wait()

    return pl.pallas_call(
        kernel,
        in_specs=[STAYS] * 2,
        out_specs=pl.BlockSpec(memory_space=pl.ANY),
        out_shape=jax.ShapeDtypeStruct((2 * rows, width), f32),
        scratch_shapes=[pltpu.SemaphoreType.DMA((2,))],
        name="place",
    )(*in_vmem(mine, other))


def finish(held, held_mate, p0, p2, p3, p1, facts):
    rows, width = held.shape
    piece = rows // GROUP
    blocks = 2 * GROUP

    def kernel(held_ref, mate_ref, b0, b2, b3, b1, facts_ref, out_ref, made, sems):
        takes = row(facts_ref[...], B_ME) > 0
        core, y = core_at(), ring_at()
        copies = []
        for side, (whose, kept) in enumerate(((core, held_ref), (1 - core, mate_ref))):
            for d, src in enumerate((b0, b1, b2, b3)):
                at = pl.multiple_of((y + GROUP - d) % GROUP * piece, 8)
                block = side * GROUP + d
                made[block] = jnp.where(takes, src[side * piece : (side + 1) * piece], kept[pl.ds(at, piece), :])
                to = out_ref.at[pl.ds(pl.multiple_of(whose * rows + at, 8), piece), :]
                copies.append(pltpu.make_async_copy(made.at[block], to, sems.at[block]))
                copies[-1].start()
        for copy in copies:
            copy.wait()

    return pl.pallas_call(
        kernel,
        in_specs=[STAYS] * 7,
        out_specs=pl.BlockSpec(memory_space=pl.ANY),
        out_shape=jax.ShapeDtypeStruct((2 * rows, width), f32),
        scratch_shapes=[pltpu.VMEM((blocks, piece, width), f32), pltpu.SemaphoreType.DMA((blocks,))],
        compiler_params=pltpu.CompilerParams(vmem_limit_bytes=8 << 20),
        name="finish",
    )(*in_vmem(held, held_mate, p0, p2, p3, p1, facts))


def ring(step):
    size = lax.axis_size("col")
    return [(i, i - i % GROUP + (i + step) % GROUP) for i in range(size)]


def swap(bit):
    return [(i, i ^ bit) for i in range(lax.axis_size("row"))]


def to_mate(x):
    return lax.ppermute(x, "row", swap(1))


def to_far(x):
    return lax.ppermute(x, "row", swap(2))


def around(x2, x1, x3):
    return [lax.ppermute(x, "col", ring(d)) for d, x in zip(DISTANCES, (x2, x1, x3))]


def after(x, *done):
    return lax.optimization_barrier((x, *done))[0]


def per_device(features, values, out_grad, query_weight, key_weight, query_mean, query_square, key_mean, key_square, members):
    f, v, o, wq, wk = [a[0, 0] for a in (features, values, out_grad, query_weight, key_weight)]
    mq, sq, mk, sk = [a[0, 0] for a in (query_mean, query_square, key_mean, key_square)]

    mine0, other0, facts, ds, queries, ft = query_step(members, f, v, o, wq, wk, mq, sq)
    theirs0 = to_mate(other0)
    part0, facts = chip_sum(mine0, theirs0, facts, True)
    far0 = to_far(part0)
    mine1, other1 = key_step(after(ds, part0), queries, ft, wk, mk, sk)
    theirs1 = to_mate(other1)
    part1, _ = chip_sum(mine1, theirs1, facts, False)
    far1 = to_far(after(part1, far0))

    own0, s2, s1, s3, held0, held_mate0, facts = row_mean(mine0, theirs0, far0, facts, True)
    total0, facts = col_mean(own0, around(s2, s1, s3), facts, True)
    p2, p1, p3 = around(total0, total0, total0)
    query_mine, query_mate = choose(held0, held_mate0, total0, p3, p1, p2, facts)
    query_other = to_mate(query_mate)

    own1, s2, s1, s3, held1, held_mate1, _ = row_mean(mine1, theirs1, after(far1, total0), facts, False)
    got1 = around(s2, s1, s3)
    held_mate1 = to_mate(held_mate1)
    me, mate = col_mean(after(own1, query_mine), got1, facts, False)
    total1 = joined(me, to_mate(mate))
    p2, p1, p3 = around(total1, total1, total1)
    query = place(query_mine, query_other)
    key = finish(held1, held_mate1, total1, after(p2, query), p3, p1, facts)
    return query[None, None], key[None, None]


def solution(mesh):
    mats = P("row", "col", None, None)
    return jax.shard_map(
        per_device,
        mesh=mesh,
        in_specs=(mats,) * 9 + (P("row", "col", None),),
        out_specs=(mats, mats),
        check_vma=False,
    )
```

```python
import functools
import math

import jax
import jax.numpy as jnp
from jax import lax
from jax.experimental import pallas as pl
from jax.experimental.pallas import tpu as pltpu
from jax.sharding import PartitionSpec as P

HD = 64
SEQ = 512
QUAD = 256
PAIR = 128
GROUP = 4
NOTE = 8
FIRST, TURN, LAST = 160, 96, 192
bf16 = jnp.bfloat16
f32 = jnp.float32

beta_one = 0.9
beta_two = 0.999
epsilon = 1e-06
decay_rate = 0.01
learn_rate = 0.1
correction_one = 1.0 - math.exp(100.0 * math.log(0.9))
correction_two = 1.0 - math.exp(100.0 * math.log(0.999))


def dot(a, b, ca=1, cb=0):
    return lax.dot_general(a, b, (((ca,), (cb,)), ((), ())), preferred_element_type=f32)


def lamb_direction(w, m, s, g):
    first = beta_one * m + (1.0 - beta_one) * g
    second = beta_two * s + (1.0 - beta_two) * g * g
    return first / correction_one / (jnp.sqrt(second / correction_two) + epsilon) + decay_rate * w


def lamb_ratio(norms):
    w2 = jnp.full((1, 1), norms[0], f32)
    u2 = jnp.full((1, 1), norms[1], f32)
    return learn_rate * jnp.sqrt(w2) / jnp.sqrt(u2 + epsilon)


def only_head(pair, h):
    lane = lax.broadcasted_iota(jnp.int32, (1, PAIR), 1)
    return jnp.where((lane >= h * HD) & (lane < (h + 1) * HD), pair, jnp.zeros((), pair.dtype))


def core_at():
    return lax.axis_index("row") % 2


def ring_at():
    return lax.axis_index("col") % GROUP


def deal(fill, size, mines, others):
    for side, outs in ((core_at(), mines), (1 - core_at(), others)):
        at = side * (size // 2)
        for out, count in outs:
            out[:count] = fill(pl.ds(pl.multiple_of(at, 8), count))
            at = at + count


def query_kernel(
    members, f_ref, v_ref, o_ref, wq_ref, wk_ref, m_ref, s_ref,
    mine_ref, turn_ref, other_ref, facts_ref, ds_ref, q_ref, ft_ref, ks, kt, gqt, u_all, w_all, norms,
):
    step = pl.program_id(0)
    last = pl.num_programs(0) - 1
    tokens, width = f_ref.shape
    in_scale = 1.0 / math.sqrt(width)
    soft_scale = math.log2(math.e) / math.sqrt(HD)
    cols = pl.ds(pl.multiple_of(step * QUAD, QUAD), QUAD)

    @pl.when(step == 0)
    def _():
        ft_ref[...] = f_ref[...].T
        norms[0] = 0.0
        norms[1] = 0.0

    feats = f_ref[...]
    queries = (dot(feats, wq_ref[...].astype(bf16)) * in_scale).astype(bf16)
    q_ref[:, cols] = queries
    keys = (dot(feats, wk_ref[...].astype(bf16)) * in_scale).astype(bf16)
    ks[...] = keys
    kt[...] = keys.T
    units = [(s, head) for s in range(tokens // SEQ) for head in range(0, QUAD, HD)]

    def products(s, head):
        rows = slice(s * SEQ, (s + 1) * SEQ)
        lanes = slice(head // PAIR * PAIR, head // PAIR * PAIR + PAIR)
        h = head % PAIR // HD
        o_head = only_head(o_ref[rows, lanes], h) * (1.0 / math.sqrt(HD))
        scores = dot(ks[rows, lanes], only_head(queries[rows, lanes], h), 1, 1)
        return scores, dot(v_ref[rows, lanes], o_head.astype(bf16), 1, 1)

    ready = products(*units[0])
    for i, (s, head) in enumerate(units):
        rows = slice(s * SEQ, (s + 1) * SEQ)
        scores, grad_prob = ready
        if i + 1 < len(units):
            ready = products(*units[i + 1])
        top = jnp.max(scores, axis=0, keepdims=True)
        e = jnp.exp2((scores - top) * soft_scale)
        prob = e * (1.0 / jnp.sum(e, axis=0, keepdims=True))
        prob_low = prob.astype(bf16).astype(f32)
        delta = jnp.sum(prob_low * grad_prob, axis=0, keepdims=True)
        grad_score = (prob * (grad_prob - delta)).astype(bf16)
        ds_ref[step * (QUAD // HD) + head // HD, rows, :] = grad_score
        gqt[head : head + HD, rows] = dot(kt[head : head + HD, rows], grad_score).astype(bf16)
    grad = dot(ft_ref[...], gqt[...], 1, 1) * in_scale
    w = wq_ref[...]
    u = lamb_direction(w, m_ref[...], s_ref[...], grad)
    u_all[:, cols] = u
    w_all[:, cols] = w
    norms[0] += jnp.sum(w * w)
    norms[1] += jnp.sum(u * u)

    @pl.when(step == last)
    def _():
        ratio = lamb_ratio(norms)
        new = lambda here: w_all[here, :] - ratio * u_all[here, :]
        deal(new, width, ((mine_ref, FIRST), (turn_ref, TURN)), ((other_ref, width // 2),))
        at = lax.broadcasted_iota(jnp.int32, facts_ref.shape, 0)
        facts = jnp.where(at == 0, members[0, 0, 0], jnp.where(at == 1, members[0, 0, 1], 0)).astype(f32)
        facts_ref[...] = facts
        other_ref[width // 2 :] = facts


def key_kernel(
    ds_ref, q_ref, ft_ref, turn_ref, w_ref, m_ref, s_ref,
    turned_ref, mine_ref, turned_other, other_ref, gks, u_all, w_all, norms,
):
    step = pl.program_id(0)
    last = pl.num_programs(0) - 1
    tokens, width = q_ref.shape
    in_scale = 1.0 / math.sqrt(width)
    cols = pl.ds(pl.multiple_of(step * QUAD, QUAD), QUAD)

    @pl.when(step == 0)
    def _():
        norms[0] = 0.0
        norms[1] = 0.0

    for s in range(tokens // SEQ):
        rows = slice(s * SEQ, (s + 1) * SEQ)
        for p in range(QUAD // PAIR):
            lanes = pl.ds(pl.multiple_of(step * QUAD + p * PAIR, PAIR), PAIR)
            pair = q_ref[rows, lanes]
            grad = jnp.zeros((SEQ, PAIR), f32)
            for h in range(PAIR // HD):
                unit = step * (QUAD // HD) + p * (PAIR // HD) + h
                grad = grad + dot(ds_ref[unit, rows, :], only_head(pair, h))
            gks[rows, p * PAIR : (p + 1) * PAIR] = grad.astype(bf16)
    grad = dot(ft_ref[...], gks[...]) * in_scale
    w = w_ref[...]
    u = lamb_direction(w, m_ref[...], s_ref[...], grad)
    u_all[:, cols] = u
    w_all[:, cols] = w
    norms[0] += jnp.sum(w * w)
    norms[1] += jnp.sum(u * u)

    @pl.when(step == last)
    def _():
        ratio = lamb_ratio(norms)
        new = lambda here: w_all[here, :] - ratio * u_all[here, :]
        turned_ref[:TURN] = turn_ref[...]
        keys = width // 2 - LAST
        mines = ((turned_ref.at[TURN:], keys), (mine_ref, LAST))
        deal(new, width, mines, ((turned_other, keys), (other_ref, LAST)))


SCALARS = pl.BlockSpec(memory_space=pltpu.SMEM)
STAYS = pl.BlockSpec(memory_space=pltpu.VMEM)


def in_hbm(*xs):
    return [pltpu.with_memory_space_constraint(x, pltpu.HBM) for x in xs]


def in_vmem(*xs):
    return [pltpu.with_memory_space_constraint(x, pltpu.VMEM) for x in xs]


def query_step(members, f, v, o, wq, wk, m, s):
    tokens, width = f.shape
    heads = wq.shape[1]
    tok = pl.BlockSpec((tokens, QUAD), lambda i: (0, i))
    mat = pl.BlockSpec((width, QUAD), lambda i: (0, i))
    full = pl.BlockSpec((tokens, width), lambda i: (0, 0))
    shapes = [(FIRST, heads), (TURN, heads), (width // 2 + NOTE, heads), (NOTE, heads)]
    return pl.pallas_call(
        query_kernel,
        grid=(heads // QUAD,),
        in_specs=[SCALARS, full, tok, tok, mat, mat, mat, mat],
        out_specs=[STAYS] * 7,
        out_shape=[pltpu.VMEM(x, f32) for x in shapes]
        + [pltpu.VMEM(x, bf16) for x in ((heads // HD, tokens, SEQ), (tokens, heads), (width, tokens))],
        scratch_shapes=[
            pltpu.VMEM((tokens, QUAD), bf16),
            pltpu.VMEM((QUAD, tokens), bf16),
            pltpu.VMEM((QUAD, tokens), bf16),
            pltpu.VMEM((width, heads), f32),
            pltpu.VMEM((width, heads), f32),
            pltpu.SMEM((2,), f32),
        ],
        compiler_params=pltpu.CompilerParams(vmem_limit_bytes=36 << 20),
        name="query_step",
    )(*in_hbm(members, f, v, o, wq, wk, m, s))


def key_step(ds, q, ft, turn, w, m, s):
    tokens, heads = q.shape
    width = ft.shape[0]
    keys = width // 2 - LAST
    mat = pl.BlockSpec((width, QUAD), lambda i: (0, i))
    return pl.pallas_call(
        key_kernel,
        grid=(heads // QUAD,),
        in_specs=[STAYS] * 4 + [mat, mat, mat],
        out_specs=[STAYS] * 4,
        out_shape=[pltpu.VMEM((r, heads), f32) for r in (TURN + keys, LAST, keys, LAST)],
        scratch_shapes=[
            pltpu.VMEM((tokens, QUAD), bf16),
            pltpu.VMEM((width, heads), f32),
            pltpu.VMEM((width, heads), f32),
            pltpu.SMEM((2,), f32),
        ],
        compiler_params=pltpu.CompilerParams(vmem_limit_bytes=24 << 20),
        name="key_step",
    )(*in_vmem(ds, q, ft, turn), *in_hbm(w, m, s))


A_ME, B_ME, A_MATE, B_MATE, A_CHIP, A_COUNT, B_COUNT, B_COUNT_MATE = range(8)
DISTANCES = (2, 1, 3)
NO_HBM = pl.CostEstimate(flops=0, transcendentals=0, bytes_accessed=0)


def small_call(kernel, name, shapes, *operands):
    got = pl.pallas_call(
        kernel,
        in_specs=[STAYS] * len(operands),
        out_specs=[STAYS] * len(shapes),
        out_shape=[pltpu.VMEM(s, f32) for s in shapes],
        compiler_params=pltpu.CompilerParams(vmem_limit_bytes=8 << 20),
        cost_estimate=NO_HBM,
        name=name,
    )(*in_vmem(*operands))
    return list(got)


def row(facts, i):
    return facts[i : i + 1, :]


def chip_sum(mine, theirs, facts):
    rows, width = mine.shape

    def kernel(mine_ref, theirs_ref, facts_ref, out_ref, facts_out):
        f = facts_ref[...]
        got = theirs_ref[theirs_ref.shape[0] - NOTE :]
        at = lax.broadcasted_iota(jnp.int32, f.shape, 0)
        f = jnp.where(at == A_MATE, row(got, 0), jnp.where(at == B_MATE, row(got, 1), f))
        f = jnp.where(at == A_CHIP, row(f, A_ME) + row(f, A_MATE), f)
        out_ref[rows:] = f
        facts_out[...] = f
        out_ref[:rows] = row(f, A_ME) * mine_ref[...] + row(f, A_MATE) * theirs_ref[:rows]

    return small_call(kernel, "chip_sum", [(rows + NOTE, width), facts.shape], mine, theirs, facts)


def chip_sum_turned(turned, theirs_query, theirs_key, facts):
    rows, width = turned.shape

    def kernel(turned_ref, tq_ref, tk_ref, facts_ref, out_ref, theirs_out):
        f = facts_ref[...]
        theirs_out[:TURN] = tq_ref[FIRST : FIRST + TURN]
        theirs_out[TURN:] = tk_ref[...]
        out_ref[:rows] = row(f, A_ME) * turned_ref[...] + row(f, A_MATE) * theirs_out[...]
        out_ref[rows : rows + NOTE] = f
        out_ref[rows + NOTE :] = f

    shapes = [(rows + 2 * NOTE, width), (rows, width)]
    return small_call(kernel, "chip_sum_turned", shapes, turned, theirs_query, theirs_key, facts)


def chip_sum_last(mine, theirs, facts):
    rows, width = mine.shape

    def kernel(mine_ref, theirs_ref, facts_ref, out_ref):
        f = facts_ref[...]
        out_ref[:rows] = row(f, A_ME) * mine_ref[...] + row(f, A_MATE) * theirs_ref[...]
        out_ref[rows:] = f

    return small_call(kernel, "chip_sum_last", [(rows + NOTE, width)], mine, theirs, facts)[0]


def row_mean(mine, theirs, far, facts, first):
    rows, width = mine.shape
    piece = rows // GROUP

    def kernel(mine_ref, theirs_ref, far_ref, facts_ref, own, s2, s1, s3, held, held_mate, *maybe_facts):
        f = facts_ref[...]
        if first:
            at = lax.broadcasted_iota(jnp.int32, f.shape, 0)
            count = row(f, A_CHIP) + row(far_ref[rows : rows + NOTE], A_CHIP)
            f = jnp.where(at == A_COUNT, jnp.maximum(count, 1.0), f)
            maybe_facts[0][...] = f
        y = ring_at()
        for d, out in enumerate((own, s1, s2, s3)):
            here = pl.ds(pl.multiple_of((y + d) % GROUP * piece, 8), piece)
            m, t = mine_ref[here, :], theirs_ref[here, :]
            mean = (row(f, A_ME) * m + row(f, A_MATE) * t + far_ref[here, :]) / row(f, A_COUNT)
            m = jnp.where(row(f, A_ME) > 0, mean, m)
            t = jnp.where(row(f, A_MATE) > 0, mean, t)
            held[here, :] = m
            held_mate[here, :] = t
            out[:piece] = m * row(f, B_ME)
            out[piece : 2 * piece] = t * row(f, B_MATE)
            if first and d:
                out[2 * piece :] = f

    sent = (2 * piece + (NOTE if first else 0), width)
    shapes = [(2 * piece, width), sent, sent, sent, (rows, width), (rows, width)]
    if first:
        shapes = shapes + [facts.shape]
    got = small_call(kernel, "row_mean", shapes, mine, theirs, far, facts)
    return got if first else got + [facts]


def col_mean(own, got, facts, first=False, split=False):
    rows, width = own.shape
    piece = rows // 2

    def kernel(own_ref, g1, g2, g3, facts_ref, *outs):
        f = facts_ref[...]
        if first:
            at = lax.broadcasted_iota(jnp.int32, f.shape, 0)
            notes = [g[rows:] for g in (g1, g2, g3)]
            count = sum([row(n, B_ME) for n in notes], row(f, B_ME))
            count_mate = sum([row(n, B_MATE) for n in notes], row(f, B_MATE))
            f = jnp.where(at == B_COUNT, jnp.maximum(count, 1.0), f)
            f = jnp.where(at == B_COUNT_MATE, jnp.maximum(count_mate, 1.0), f)
            outs[1][...] = f
        total = own_ref[...] + g1[:rows] + g2[:rows] + g3[:rows]
        mate = outs[1] if split else outs[0].at[piece:]
        outs[0][:piece] = total[:piece] / row(f, B_COUNT)
        mate[...] = total[piece:] / row(f, B_COUNT_MATE)

    shapes = [(piece, width)] * 2 if split else [(rows, width)]
    return small_call(kernel, "col_mean", shapes + ([facts.shape] if first else []), own, *got, facts)


def joined(me, mate):
    piece, width = me.shape

    def kernel(me_ref, mate_ref, out):
        out[:piece] = me_ref[...]
        out[piece:] = mate_ref[...]

    return small_call(kernel, "joined", [(2 * piece, width)], me, mate)[0]


def choose(held, held_mate, p0, p3, p1, p2, facts):
    rows, width = held.shape
    piece = rows // GROUP

    def kernel(held_ref, held_mate_ref, b0, b3, b1, b2, facts_ref, me, mate):
        f = facts_ref[...]
        for d, src in enumerate((b0, b1, b2, b3)):
            here = pl.ds(pl.multiple_of((ring_at() + GROUP - d) % GROUP * piece, 8), piece)
            me[here, :] = jnp.where(row(f, B_ME) > 0, src[:piece], held_ref[here, :])
            mate[here, :] = jnp.where(row(f, B_MATE) > 0, src[piece:], held_mate_ref[here, :])

    return small_call(kernel, "choose", [(rows, width)] * 2, held, held_mate, p0, p3, p1, p2, facts)


def place(size, mine, other, turned, turned_other):
    width = mine.shape[1]

    def kernel(mine_ref, other_ref, turned_ref, turned_other_ref, out_ref, sems):
        copies = []
        for a, b, side in ((mine_ref, turned_ref, core_at()), (other_ref, turned_other_ref, 1 - core_at())):
            for src, skip, count in ((a, 0, FIRST), (b, FIRST, TURN)):
                to = out_ref.at[pl.ds(pl.multiple_of(side * (size // 2) + skip, 8), count), :]
                copies.append(pltpu.make_async_copy(src.at[:count], to, sems.at[len(copies)]))
                copies[-1].start()
        for copy in copies:
            copy.wait()

    return pl.pallas_call(
        kernel,
        in_specs=[STAYS] * 4,
        out_specs=pl.BlockSpec(memory_space=pl.ANY),
        out_shape=jax.ShapeDtypeStruct((size, width), f32),
        scratch_shapes=[pltpu.SemaphoreType.DMA((4,))],
        name="place",
    )(*in_vmem(mine, other, turned, turned_other))


def finish(size, turned, turned_other, held, held_mate, p0, p2, p3, p1, facts):
    rows, width = held.shape
    piece = rows // GROUP
    blocks = 2 * GROUP
    keys = size // 2 - rows

    def kernel(turned_ref, turned_other_ref, held_ref, mate_ref, b0, b2, b3, b1, facts_ref, out_ref, made, sems):
        takes = row(facts_ref[...], B_ME) > 0
        y = ring_at()
        copies = []
        sides = ((core_at(), turned_ref, held_ref), (1 - core_at(), turned_other_ref, mate_ref))
        for side, (whose, early, kept) in enumerate(sides):
            base = whose * (size // 2)
            to = out_ref.at[pl.ds(pl.multiple_of(base, 8), keys), :]
            copies.append(pltpu.make_async_copy(early.at[TURN:], to, sems.at[len(copies)]))
            copies[-1].start()
            for d, src in enumerate((b0, b1, b2, b3)):
                at = pl.multiple_of((y + GROUP - d) % GROUP * piece, 8)
                block = side * GROUP + d
                made[block] = jnp.where(takes, src[side * piece : (side + 1) * piece], kept[pl.ds(at, piece), :])
                to = out_ref.at[pl.ds(pl.multiple_of(base + keys + at, 8), piece), :]
                copies.append(pltpu.make_async_copy(made.at[block], to, sems.at[len(copies)]))
                copies[-1].start()
        for copy in copies:
            copy.wait()

    return pl.pallas_call(
        kernel,
        in_specs=[STAYS] * 9,
        out_specs=pl.BlockSpec(memory_space=pl.ANY),
        out_shape=jax.ShapeDtypeStruct((size, width), f32),
        scratch_shapes=[pltpu.VMEM((blocks, piece, width), f32), pltpu.SemaphoreType.DMA((blocks + 2,))],
        compiler_params=pltpu.CompilerParams(vmem_limit_bytes=8 << 20),
        name="finish",
    )(*in_vmem(turned, turned_other, held, held_mate, p0, p2, p3, p1, facts))


def ring(step):
    size = lax.axis_size("col")
    return [(i, i - i % GROUP + (i + step) % GROUP) for i in range(size)]


def swap(bit):
    return [(i, i ^ bit) for i in range(lax.axis_size("row"))]


def to_mate(x):
    return lax.ppermute(x, "row", swap(1))


def to_far(x):
    return lax.ppermute(x, "row", swap(2))


def around(x2, x1, x3):
    return [lax.ppermute(x, "col", ring(d)) for d, x in zip(DISTANCES, (x2, x1, x3))]


def after(x, *done):
    return lax.optimization_barrier((x, *done))[0]


def per_device(features, values, out_grad, query_weight, key_weight, query_mean, query_square, key_mean, key_square, members):
    f, v, o, wq, wk = [a[0, 0] for a in (features, values, out_grad, query_weight, key_weight)]
    mq, sq, mk, sk = [a[0, 0] for a in (query_mean, query_square, key_mean, key_square)]

    size = wq.shape[0]
    mine0, turn, other0, facts, ds, queries, ft = query_step(members, f, v, o, wq, wk, mq, sq)
    theirs0 = to_mate(other0)
    part0, facts = chip_sum(mine0, theirs0, facts)
    far0 = to_far(part0)
    mine1, mine2, other1, other2 = key_step(after(ds, part0), queries, ft, turn, wk, mk, sk)
    part1, theirs1 = chip_sum_turned(mine1, theirs0, to_mate(other1), facts)
    far1 = to_far(after(part1, far0))
    theirs2 = to_mate(after(other2, far0))
    part2 = chip_sum_last(mine2, theirs2, facts)
    far2 = to_far(after(part2, far1))

    own0, s2, s1, s3, held0, held_mate0, facts = row_mean(mine0, theirs0, far0, facts, True)
    total0, facts = col_mean(own0, around(s2, s1, s3), facts, first=True)
    p2, p1, p3 = around(total0, total0, total0)
    me0, mate0 = choose(held0, held_mate0, total0, p3, p1, p2, facts)
    other0 = to_mate(mate0)

    own1, s2, s1, s3, held1, held_mate1, _ = row_mean(mine1, theirs1, after(far1, total0), facts, False)
    got1 = around(s2, s1, s3)
    total1 = col_mean(after(own1, me0), got1, facts)[0]
    p2, p1, p3 = around(total1, total1, total1)
    me1, mate1 = choose(held1, held_mate1, total1, p3, p1, p2, facts)
    other1 = to_mate(mate1)

    own2, s2, s1, s3, held2, held_mate2, _ = row_mean(mine2, theirs2, after(far2, total1), facts, False)
    got2 = around(s2, s1, s3)
    held_mate2 = to_mate(held_mate2)
    me2, mate2 = col_mean(after(own2, me1), got2, facts, split=True)
    total2 = joined(me2, to_mate(mate2))
    p2, p1, p3 = around(total2, total2, total2)
    query = place(size, me0, other0, me1, other1)
    key = finish(size, me1, other1, held2, held_mate2, total2, after(p2, query), p3, p1, facts)
    return query[None, None], key[None, None]


def solution(mesh):
    mats = P("row", "col", None, None)
    return jax.shard_map(
        per_device,
        mesh=mesh,
        in_specs=(mats,) * 9 + (P("row", "col", None),),
        out_specs=(mats, mats),
        check_vma=False,
    )
```

```python
import functools
import math

import jax
import jax.numpy as jnp
from jax import lax
from jax.experimental import pallas as pl
from jax.experimental.pallas import tpu as pltpu
from jax.sharding import PartitionSpec as P

HD = 64
SEQ = 512
QUAD = 256
PAIR = 128
GROUP = 4
NOTE = 8
FIRST, TURN, LAST = 160, 96, 192
bf16 = jnp.bfloat16
f32 = jnp.float32

beta_one = 0.9
beta_two = 0.999
epsilon = 1e-06
decay_rate = 0.01
learn_rate = 0.1
correction_one = 1.0 - math.exp(100.0 * math.log(0.9))
correction_two = 1.0 - math.exp(100.0 * math.log(0.999))


def dot(a, b, ca=1, cb=0):
    return lax.dot_general(a, b, (((ca,), (cb,)), ((), ())), preferred_element_type=f32)


def lamb_direction(w, m, s, g):
    first = beta_one * m + (1.0 - beta_one) * g
    second = beta_two * s + (1.0 - beta_two) * g * g
    return first / correction_one / (jnp.sqrt(second / correction_two) + epsilon) + decay_rate * w


def lamb_ratio(norms):
    w2 = jnp.full((1, 1), norms[0], f32)
    u2 = jnp.full((1, 1), norms[1], f32)
    return learn_rate * jnp.sqrt(w2) / jnp.sqrt(u2 + epsilon)


def only_head(pair, h):
    lane = lax.broadcasted_iota(jnp.int32, (1, PAIR), 1)
    return jnp.where((lane >= h * HD) & (lane < (h + 1) * HD), pair, jnp.zeros((), pair.dtype))


def core_at():
    return lax.axis_index("row") % 2


def ring_at():
    return lax.axis_index("col") % GROUP


def deal(fill, size, mines, others):
    for side, outs in ((core_at(), mines), (1 - core_at(), others)):
        at = side * (size // 2)
        for out, count in outs:
            out[:count] = fill(pl.ds(pl.multiple_of(at, 8), count))
            at = at + count


def query_kernel(
    members, f_ref, v_ref, o_ref, wq_ref, wk_ref, m_ref, s_ref,
    mine_ref, turn_ref, other_ref, facts_ref, ds_ref, q_ref, ft_ref, ks, kt, gqt, u_all, w_all, norms,
):
    step = pl.program_id(0)
    last = pl.num_programs(0) - 1
    tokens, width = f_ref.shape
    in_scale = 1.0 / math.sqrt(width)
    soft_scale = math.log2(math.e) / math.sqrt(HD)
    cols = pl.ds(pl.multiple_of(step * QUAD, QUAD), QUAD)

    @pl.when(step == 0)
    def _():
        ft_ref[...] = f_ref[...].T
        norms[0] = 0.0
        norms[1] = 0.0

    feats = f_ref[...]
    queries = (dot(feats, wq_ref[...].astype(bf16)) * in_scale).astype(bf16)
    q_ref[:, cols] = queries
    keys = (dot(feats, wk_ref[...].astype(bf16)) * in_scale).astype(bf16)
    ks[...] = keys
    kt[...] = keys.T
    units = [(s, head) for s in range(tokens // SEQ) for head in range(0, QUAD, HD)]

    def products(s, head):
        rows = slice(s * SEQ, (s + 1) * SEQ)
        lanes = slice(head // PAIR * PAIR, head // PAIR * PAIR + PAIR)
        h = head % PAIR // HD
        o_head = only_head(o_ref[rows, lanes], h) * (1.0 / math.sqrt(HD))
        scores = dot(ks[rows, lanes], only_head(queries[rows, lanes], h), 1, 1)
        return scores, dot(v_ref[rows, lanes], o_head.astype(bf16), 1, 1)

    ready = products(*units[0])
    for i, (s, head) in enumerate(units):
        rows = slice(s * SEQ, (s + 1) * SEQ)
        scores, grad_prob = ready
        if i + 1 < len(units):
            ready = products(*units[i + 1])
        top = jnp.max(scores, axis=0, keepdims=True)
        e = jnp.exp2((scores - top) * soft_scale)
        prob = e * (1.0 / jnp.sum(e, axis=0, keepdims=True))
        prob_low = prob.astype(bf16).astype(f32)
        delta = jnp.sum(prob_low * grad_prob, axis=0, keepdims=True)
        grad_score = (prob * (grad_prob - delta)).astype(bf16)
        ds_ref[step * (QUAD // HD) + head // HD, rows, :] = grad_score
        gqt[head : head + HD, rows] = dot(kt[head : head + HD, rows], grad_score).astype(bf16)
    grad = dot(ft_ref[...], gqt[...], 1, 1) * in_scale
    w = wq_ref[...]
    u = lamb_direction(w, m_ref[...], s_ref[...], grad)
    u_all[:, cols] = u
    w_all[:, cols] = w
    norms[0] += jnp.sum(w * w)
    norms[1] += jnp.sum(u * u)

    @pl.when(step == last)
    def _():
        ratio = lamb_ratio(norms)
        new = lambda here: w_all[here, :] - ratio * u_all[here, :]
        deal(new, width, ((mine_ref, FIRST), (turn_ref, TURN)), ((other_ref, width // 2),))
        at = lax.broadcasted_iota(jnp.int32, facts_ref.shape, 0)
        facts = jnp.where(at == 0, members[0, 0, 0], jnp.where(at == 1, members[0, 0, 1], 0)).astype(f32)
        facts_ref[...] = facts
        other_ref[width // 2 :] = facts


def key_kernel(
    ds_ref, q_ref, ft_ref, turn_ref, w_ref, m_ref, s_ref,
    turned_ref, mine_ref, turned_other, other_ref, gks, u_all, w_all, norms,
):
    step = pl.program_id(0)
    last = pl.num_programs(0) - 1
    tokens, width = q_ref.shape
    in_scale = 1.0 / math.sqrt(width)
    cols = pl.ds(pl.multiple_of(step * QUAD, QUAD), QUAD)

    @pl.when(step == 0)
    def _():
        norms[0] = 0.0
        norms[1] = 0.0

    for s in range(tokens // SEQ):
        rows = slice(s * SEQ, (s + 1) * SEQ)
        for p in range(QUAD // PAIR):
            lanes = pl.ds(pl.multiple_of(step * QUAD + p * PAIR, PAIR), PAIR)
            pair = q_ref[rows, lanes]
            grad = jnp.zeros((SEQ, PAIR), f32)
            for h in range(PAIR // HD):
                unit = step * (QUAD // HD) + p * (PAIR // HD) + h
                grad = grad + dot(ds_ref[unit, rows, :], only_head(pair, h))
            gks[rows, p * PAIR : (p + 1) * PAIR] = grad.astype(bf16)
    grad = dot(ft_ref[...], gks[...]) * in_scale
    w = w_ref[...]
    u = lamb_direction(w, m_ref[...], s_ref[...], grad)
    u_all[:, cols] = u
    w_all[:, cols] = w
    norms[0] += jnp.sum(w * w)
    norms[1] += jnp.sum(u * u)

    @pl.when(step == last)
    def _():
        ratio = lamb_ratio(norms)
        new = lambda here: w_all[here, :] - ratio * u_all[here, :]
        turned_ref[:TURN] = turn_ref[...]
        keys = width // 2 - LAST
        mines = ((turned_ref.at[TURN:], keys), (mine_ref, LAST))
        deal(new, width, mines, ((turned_other, keys), (other_ref, LAST)))


SCALARS = pl.BlockSpec(memory_space=pltpu.SMEM)
STAYS = pl.BlockSpec(memory_space=pltpu.VMEM)


def in_hbm(*xs):
    return [pltpu.with_memory_space_constraint(x, pltpu.HBM) for x in xs]


def in_vmem(*xs):
    return [pltpu.with_memory_space_constraint(x, pltpu.VMEM) for x in xs]


def query_step(members, f, v, o, wq, wk, m, s):
    tokens, width = f.shape
    heads = wq.shape[1]
    tok = pl.BlockSpec((tokens, QUAD), lambda i: (0, i))
    mat = pl.BlockSpec((width, QUAD), lambda i: (0, i))
    full = pl.BlockSpec((tokens, width), lambda i: (0, 0))
    shapes = [(FIRST, heads), (TURN, heads), (width // 2 + NOTE, heads), (NOTE, heads)]
    return pl.pallas_call(
        query_kernel,
        grid=(heads // QUAD,),
        in_specs=[SCALARS, full, tok, tok, mat, mat, mat, mat],
        out_specs=[STAYS] * 7,
        out_shape=[pltpu.VMEM(x, f32) for x in shapes]
        + [pltpu.VMEM(x, bf16) for x in ((heads // HD, tokens, SEQ), (tokens, heads), (width, tokens))],
        scratch_shapes=[
            pltpu.VMEM((tokens, QUAD), bf16),
            pltpu.VMEM((QUAD, tokens), bf16),
            pltpu.VMEM((QUAD, tokens), bf16),
            pltpu.VMEM((width, heads), f32),
            pltpu.VMEM((width, heads), f32),
            pltpu.SMEM((2,), f32),
        ],
        compiler_params=pltpu.CompilerParams(vmem_limit_bytes=36 << 20),
        name="query_step",
    )(*in_hbm(members, f, v, o, wq, wk, m, s))


def key_step(ds, q, ft, turn, w, m, s):
    tokens, heads = q.shape
    width = ft.shape[0]
    keys = width // 2 - LAST
    mat = pl.BlockSpec((width, QUAD), lambda i: (0, i))
    return pl.pallas_call(
        key_kernel,
        grid=(heads // QUAD,),
        in_specs=[STAYS] * 4 + [mat, mat, mat],
        out_specs=[STAYS] * 4,
        out_shape=[pltpu.VMEM((r, heads), f32) for r in (TURN + keys, LAST, keys, LAST)],
        scratch_shapes=[
            pltpu.VMEM((tokens, QUAD), bf16),
            pltpu.VMEM((width, heads), f32),
            pltpu.VMEM((width, heads), f32),
            pltpu.SMEM((2,), f32),
        ],
        compiler_params=pltpu.CompilerParams(vmem_limit_bytes=24 << 20),
        name="key_step",
    )(*in_vmem(ds, q, ft, turn), *in_hbm(w, m, s))


A_ME, B_ME, A_MATE, B_MATE, A_CHIP, A_COUNT, B_COUNT, B_COUNT_MATE = range(8)
DISTANCES = (2, 1, 3)
NO_HBM = pl.CostEstimate(flops=0, transcendentals=0, bytes_accessed=0)


def small_call(kernel, name, shapes, *operands):
    got = pl.pallas_call(
        kernel,
        in_specs=[STAYS] * len(operands),
        out_specs=[STAYS] * len(shapes),
        out_shape=[pltpu.VMEM(s, f32) for s in shapes],
        compiler_params=pltpu.CompilerParams(vmem_limit_bytes=8 << 20),
        cost_estimate=NO_HBM,
        name=name,
    )(*in_vmem(*operands))
    return list(got)


def row(facts, i):
    return facts[i : i + 1, :]


def chip_sum(mine, theirs, facts):
    rows, width = mine.shape

    def kernel(mine_ref, theirs_ref, facts_ref, out_ref, facts_out):
        f = facts_ref[...]
        got = theirs_ref[theirs_ref.shape[0] - NOTE :]
        at = lax.broadcasted_iota(jnp.int32, f.shape, 0)
        f = jnp.where(at == A_MATE, row(got, 0), jnp.where(at == B_MATE, row(got, 1), f))
        f = jnp.where(at == A_CHIP, row(f, A_ME) + row(f, A_MATE), f)
        out_ref[rows:] = f
        facts_out[...] = f
        out_ref[:rows] = row(f, A_ME) * mine_ref[...] + row(f, A_MATE) * theirs_ref[:rows]

    return small_call(kernel, "chip_sum", [(rows + NOTE, width), facts.shape], mine, theirs, facts)


def chip_sum_turned(turned, theirs_query, theirs_key, facts):
    rows, width = turned.shape

    def kernel(turned_ref, tq_ref, tk_ref, facts_ref, out_ref, theirs_out):
        f = facts_ref[...]
        theirs_out[:TURN] = tq_ref[FIRST : FIRST + TURN]
        theirs_out[TURN:] = tk_ref[...]
        out_ref[...] = row(f, A_ME) * turned_ref[...] + row(f, A_MATE) * theirs_out[...]

    shapes = [(rows, width), (rows, width)]
    return small_call(kernel, "chip_sum_turned", shapes, turned, theirs_query, theirs_key, facts)


def chip_sum_last(mine, theirs, facts):
    rows, width = mine.shape

    def kernel(mine_ref, theirs_ref, facts_ref, out_ref):
        f = facts_ref[...]
        out_ref[...] = row(f, A_ME) * mine_ref[...] + row(f, A_MATE) * theirs_ref[...]

    return small_call(kernel, "chip_sum_last", [(rows, width)], mine, theirs, facts)[0]


def row_mean(mine, theirs, far, facts, first):
    rows, width = mine.shape
    piece = rows // GROUP

    def kernel(mine_ref, theirs_ref, far_ref, facts_ref, own, s2, s1, s3, held, held_mate, *maybe_facts):
        f = facts_ref[...]
        if first:
            at = lax.broadcasted_iota(jnp.int32, f.shape, 0)
            count = row(f, A_CHIP) + row(far_ref[rows : rows + NOTE], A_CHIP)
            f = jnp.where(at == A_COUNT, jnp.maximum(count, 1.0), f)
            maybe_facts[0][...] = f
        y = ring_at()
        for d, out in enumerate((own, s1, s2, s3)):
            here = pl.ds(pl.multiple_of((y + d) % GROUP * piece, 8), piece)
            m, t = mine_ref[here, :], theirs_ref[here, :]
            mean = (row(f, A_ME) * m + row(f, A_MATE) * t + far_ref[here, :]) / row(f, A_COUNT)
            m = jnp.where(row(f, A_ME) > 0, mean, m)
            t = jnp.where(row(f, A_MATE) > 0, mean, t)
            held[here, :] = m
            held_mate[here, :] = t
            out[:piece] = m * row(f, B_ME)
            out[piece:] = t * row(f, B_MATE)

    shapes = [(2 * piece, width)] * 4 + [(rows, width)] * 2
    if first:
        shapes = shapes + [facts.shape]
    got = small_call(kernel, "row_mean", shapes, mine, theirs, far, facts)
    return got if first else got + [facts]


def col_sum(own, got, facts):
    rows, width = own.shape

    def kernel(own_ref, g1, g2, g3, facts_ref, out):
        out[:rows] = own_ref[...] + g1[...] + g2[...] + g3[...]
        out[rows:] = facts_ref[...]

    return small_call(kernel, "col_sum", [(rows + NOTE, width)], own, *got, facts)[0]


def col_mean(own, got, facts, split=False):
    rows, width = own.shape
    piece = rows // 2

    def kernel(own_ref, g1, g2, g3, facts_ref, *outs):
        f = facts_ref[...]
        total = own_ref[...] + g1[...] + g2[...] + g3[...]
        mate = outs[1] if split else outs[0].at[piece:]
        outs[0][:piece] = total[:piece] / row(f, B_COUNT)
        mate[...] = total[piece:] / row(f, B_COUNT_MATE)

    shapes = [(piece, width)] * 2 if split else [(rows, width)]
    return small_call(kernel, "col_mean", shapes, own, *got, facts)


def joined(me, mate):
    piece, width = me.shape

    def kernel(me_ref, mate_ref, out):
        out[:piece] = me_ref[...]
        out[piece:] = mate_ref[...]

    return small_call(kernel, "joined", [(2 * piece, width)], me, mate)[0]


def choose(held, held_mate, p0, p3, p1, p2, facts, first):
    rows, width = held.shape
    piece = rows // GROUP

    def kernel(held_ref, held_mate_ref, b0, b3, b1, b2, facts_ref, me, mate, *maybe_facts):
        f = facts_ref[...]
        if first:
            notes = [b[2 * piece :] for b in (b1, b2, b3)]
            count = sum([row(n, B_ME) for n in notes], row(f, B_ME))
            count_mate = sum([row(n, B_MATE) for n in notes], row(f, B_MATE))
            over, over_mate = jnp.maximum(count, 1.0), jnp.maximum(count_mate, 1.0)
            at = lax.broadcasted_iota(jnp.int32, f.shape, 0)
            maybe_facts[0][...] = jnp.where(at == B_COUNT, over, jnp.where(at == B_COUNT_MATE, over_mate, f))
        for d, src in enumerate((b0, b1, b2, b3)):
            here = pl.ds(pl.multiple_of((ring_at() + GROUP - d) % GROUP * piece, 8), piece)
            mine, theirs = src[:piece], src[piece : 2 * piece]
            if first:
                mine, theirs = mine / over, theirs / over_mate
            me[here, :] = jnp.where(row(f, B_ME) > 0, mine, held_ref[here, :])
            mate[here, :] = jnp.where(row(f, B_MATE) > 0, theirs, held_mate_ref[here, :])

    shapes = [(rows, width)] * 2 + ([facts.shape] if first else [])
    return small_call(kernel, "choose", shapes, held, held_mate, p0, p3, p1, p2, facts)


def place(size, mine, other, turned, turned_other):
    width = mine.shape[1]

    def kernel(mine_ref, other_ref, turned_ref, turned_other_ref, out_ref, sems):
        copies = []
        for a, b, side in ((mine_ref, turned_ref, core_at()), (other_ref, turned_other_ref, 1 - core_at())):
            for src, skip, count in ((a, 0, FIRST), (b, FIRST, TURN)):
                to = out_ref.at[pl.ds(pl.multiple_of(side * (size // 2) + skip, 8), count), :]
                copies.append(pltpu.make_async_copy(src.at[:count], to, sems.at[len(copies)]))
                copies[-1].start()
        for copy in copies:
            copy.wait()

    return pl.pallas_call(
        kernel,
        in_specs=[STAYS] * 4,
        out_specs=pl.BlockSpec(memory_space=pl.ANY),
        out_shape=jax.ShapeDtypeStruct((size, width), f32),
        scratch_shapes=[pltpu.SemaphoreType.DMA((4,))],
        name="place",
    )(*in_vmem(mine, other, turned, turned_other))


def finish(size, turned, turned_other, held, held_mate, p0, p2, p3, p1, facts):
    rows, width = held.shape
    piece = rows // GROUP
    blocks = 2 * GROUP
    keys = size // 2 - rows

    def kernel(turned_ref, turned_other_ref, held_ref, mate_ref, b0, b2, b3, b1, facts_ref, out_ref, made, sems):
        takes = row(facts_ref[...], B_ME) > 0
        y = ring_at()
        copies = []
        sides = ((core_at(), turned_ref, held_ref), (1 - core_at(), turned_other_ref, mate_ref))
        for side, (whose, early, kept) in enumerate(sides):
            base = whose * (size // 2)
            to = out_ref.at[pl.ds(pl.multiple_of(base, 8), keys), :]
            copies.append(pltpu.make_async_copy(early.at[TURN:], to, sems.at[len(copies)]))
            copies[-1].start()
            for d, src in enumerate((b0, b1, b2, b3)):
                at = pl.multiple_of((y + GROUP - d) % GROUP * piece, 8)
                block = side * GROUP + d
                made[block] = jnp.where(takes, src[side * piece : (side + 1) * piece], kept[pl.ds(at, piece), :])
                to = out_ref.at[pl.ds(pl.multiple_of(base + keys + at, 8), piece), :]
                copies.append(pltpu.make_async_copy(made.at[block], to, sems.at[len(copies)]))
                copies[-1].start()
        for copy in copies:
            copy.wait()

    return pl.pallas_call(
        kernel,
        in_specs=[STAYS] * 9,
        out_specs=pl.BlockSpec(memory_space=pl.ANY),
        out_shape=jax.ShapeDtypeStruct((size, width), f32),
        scratch_shapes=[pltpu.VMEM((blocks, piece, width), f32), pltpu.SemaphoreType.DMA((blocks + 2,))],
        compiler_params=pltpu.CompilerParams(vmem_limit_bytes=8 << 20),
        name="finish",
    )(*in_vmem(turned, turned_other, held, held_mate, p0, p2, p3, p1, facts))


def ring(step):
    size = lax.axis_size("col")
    return [(i, i - i % GROUP + (i + step) % GROUP) for i in range(size)]


def swap(bit):
    return [(i, i ^ bit) for i in range(lax.axis_size("row"))]


def to_mate(x):
    return lax.ppermute(x, "row", swap(1))


def to_far(x):
    return lax.ppermute(x, "row", swap(2))


def around(x2, x1, x3):
    return [lax.ppermute(x, "col", ring(d)) for d, x in zip(DISTANCES, (x2, x1, x3))]


def after(x, *done):
    return lax.optimization_barrier((x, *done))[0]


def per_device(features, values, out_grad, query_weight, key_weight, query_mean, query_square, key_mean, key_square, members):
    f, v, o, wq, wk = [a[0, 0] for a in (features, values, out_grad, query_weight, key_weight)]
    mq, sq, mk, sk = [a[0, 0] for a in (query_mean, query_square, key_mean, key_square)]

    size = wq.shape[0]
    mine0, turn, other0, facts, ds, queries, ft = query_step(members, f, v, o, wq, wk, mq, sq)
    theirs0 = to_mate(other0)
    part0, facts = chip_sum(mine0, theirs0, facts)
    far0 = to_far(part0)
    mine1, mine2, other1, other2 = key_step(after(ds, part0), queries, ft, turn, wk, mk, sk)
    part1, theirs1 = chip_sum_turned(mine1, theirs0, to_mate(other1), facts)
    far1 = to_far(after(part1, far0))
    theirs2 = to_mate(after(other2, far0))
    part2 = chip_sum_last(mine2, theirs2, facts)
    far2 = to_far(after(part2, far1))

    own0, s2, s1, s3, held0, held_mate0, facts = row_mean(mine0, theirs0, far0, facts, True)
    total0 = col_sum(own0, around(s2, s1, s3), facts)
    p2, p1, p3 = around(total0, total0, total0)
    me0, mate0, counted = choose(held0, held_mate0, total0, p3, p1, p2, facts, True)
    other0 = to_mate(mate0)

    own1, s2, s1, s3, held1, held_mate1, _ = row_mean(mine1, theirs1, after(far1, total0), facts, False)
    got1 = around(s2, s1, s3)
    total1 = col_mean(after(own1, me0), got1, counted)[0]
    p2, p1, p3 = around(total1, total1, total1)
    me1, mate1 = choose(held1, held_mate1, total1, p3, p1, p2, facts, False)
    other1 = to_mate(mate1)

    own2, s2, s1, s3, held2, held_mate2, _ = row_mean(mine2, theirs2, after(far2, total1), facts, False)
    got2 = around(s2, s1, s3)
    held_mate2 = to_mate(held_mate2)
    me2, mate2 = col_mean(after(own2, me1), got2, counted, split=True)
    total2 = joined(me2, to_mate(mate2))
    p2, p1, p3 = around(total2, total2, total2)
    query = place(size, me0, other0, me1, other1)
    key = finish(size, me1, other1, held2, held_mate2, total2, after(p2, query), p3, p1, facts)
    return query[None, None], key[None, None]


def solution(mesh):
    mats = P("row", "col", None, None)
    return jax.shard_map(
        per_device,
        mesh=mesh,
        in_specs=(mats,) * 9 + (P("row", "col", None),),
        out_specs=(mats, mats),
        check_vma=False,
    )
```

```python
import functools
import math

import jax
import jax.numpy as jnp
from jax import lax
from jax.experimental import pallas as pl
from jax.experimental.pallas import tpu as pltpu
from jax.sharding import PartitionSpec as P

HD = 64
SEQ = 512
QUAD = 256
PAIR = 128
GROUP = 4
NOTE = 8
FIRST, TURN, LAST = 160, 96, 192
bf16 = jnp.bfloat16
f32 = jnp.float32

beta_one = 0.9
beta_two = 0.999
epsilon = 1e-06
decay_rate = 0.01
learn_rate = 0.1
correction_one = 1.0 - math.exp(100.0 * math.log(0.9))
correction_two = 1.0 - math.exp(100.0 * math.log(0.999))


def dot(a, b, ca=1, cb=0):
    return lax.dot_general(a, b, (((ca,), (cb,)), ((), ())), preferred_element_type=f32)


def lamb_direction(w, m, s, g):
    first = beta_one * m + (1.0 - beta_one) * g
    second = beta_two * s + (1.0 - beta_two) * g * g
    return first / correction_one / (jnp.sqrt(second / correction_two) + epsilon) + decay_rate * w


def lamb_ratio(norms):
    w2 = jnp.full((1, 1), norms[0], f32)
    u2 = jnp.full((1, 1), norms[1], f32)
    return learn_rate * jnp.sqrt(w2) / jnp.sqrt(u2 + epsilon)


def only_head(pair, h):
    lane = lax.broadcasted_iota(jnp.int32, (1, PAIR), 1)
    return jnp.where((lane >= h * HD) & (lane < (h + 1) * HD), pair, jnp.zeros((), pair.dtype))


def core_at():
    return lax.axis_index("row") % 2


def ring_at():
    return lax.axis_index("col") % GROUP


def deal(fill, size, mines, others):
    for side, outs in ((core_at(), mines), (1 - core_at(), others)):
        at = side * (size // 2)
        for out, count in outs:
            out[:count] = fill(pl.ds(pl.multiple_of(at, 8), count))
            at = at + count


def query_kernel(
    members, f_ref, v_ref, o_ref, wq_ref, wk_ref, m_ref, s_ref,
    mine_ref, turn_ref, other_ref, facts_ref, ds_ref, q_ref, ft_ref, ks, kt, gqt, u_all, w_all, norms, qt, ot,
):
    step = pl.program_id(0)
    last = pl.num_programs(0) - 1
    tokens, width = f_ref.shape
    in_scale = 1.0 / math.sqrt(width)
    soft_scale = math.log2(math.e) / math.sqrt(HD)
    cols = pl.ds(pl.multiple_of(step * QUAD, QUAD), QUAD)

    @pl.when(step == 0)
    def _():
        ft_ref[...] = f_ref[...].T
        norms[0] = 0.0
        norms[1] = 0.0

    feats = f_ref[...]
    queries = (dot(feats, wq_ref[...].astype(bf16)) * in_scale).astype(bf16)
    q_ref[:, cols] = queries
    keys = (dot(feats, wk_ref[...].astype(bf16)) * in_scale).astype(bf16)
    ks[...] = keys
    kt[...] = keys.T
    units = [(s, head) for s in range(tokens // SEQ) for head in range(0, QUAD, HD)]

    qt[...] = queries.T
    ot[...] = (o_ref[...] * (1.0 / math.sqrt(HD))).astype(bf16).T
    none = jnp.zeros((HD, SEQ), bf16)

    def products(s, head):
        rows = slice(s * SEQ, (s + 1) * SEQ)
        lanes = slice(head // PAIR * PAIR, head // PAIR * PAIR + PAIR)
        wide = lambda x: jnp.concatenate([none, x] if head % PAIR else [x, none])
        scores = dot(ks[rows, lanes], wide(qt[head : head + HD, rows]))
        return scores, dot(v_ref[rows, lanes], wide(ot[head : head + HD, rows]))

    ready = products(*units[0])
    for i, (s, head) in enumerate(units):
        rows = slice(s * SEQ, (s + 1) * SEQ)
        scores, grad_prob = ready
        if i + 1 < len(units):
            ready = products(*units[i + 1])
        top = jnp.max(scores, axis=0, keepdims=True)
        e = jnp.exp2((scores - top) * soft_scale)
        prob = e * (1.0 / jnp.sum(e, axis=0, keepdims=True))
        prob_low = prob.astype(bf16).astype(f32)
        delta = jnp.sum(prob_low * grad_prob, axis=0, keepdims=True)
        grad_score = (prob * (grad_prob - delta)).astype(bf16)
        ds_ref[step * (QUAD // HD) + head // HD, rows, :] = grad_score
        gqt[head : head + HD, rows] = dot(kt[head : head + HD, rows], grad_score).astype(bf16)
    grad = dot(ft_ref[...], gqt[...], 1, 1) * in_scale
    w = wq_ref[...]
    u = lamb_direction(w, m_ref[...], s_ref[...], grad)
    u_all[:, cols] = u
    w_all[:, cols] = w
    norms[0] += jnp.sum(w * w)
    norms[1] += jnp.sum(u * u)

    @pl.when(step == last)
    def _():
        ratio = lamb_ratio(norms)
        new = lambda here: w_all[here, :] - ratio * u_all[here, :]
        deal(new, width, ((mine_ref, FIRST), (turn_ref, TURN)), ((other_ref, width // 2),))
        at = lax.broadcasted_iota(jnp.int32, facts_ref.shape, 0)
        facts = jnp.where(at == 0, members[0, 0, 0], jnp.where(at == 1, members[0, 0, 1], 0)).astype(f32)
        facts_ref[...] = facts
        other_ref[width // 2 :] = facts


def key_kernel(
    ds_ref, q_ref, ft_ref, turn_ref, w_ref, m_ref, s_ref,
    turned_ref, mine_ref, turned_other, other_ref, gks, u_all, w_all, norms,
):
    step = pl.program_id(0)
    last = pl.num_programs(0) - 1
    tokens, width = q_ref.shape
    in_scale = 1.0 / math.sqrt(width)
    cols = pl.ds(pl.multiple_of(step * QUAD, QUAD), QUAD)

    @pl.when(step == 0)
    def _():
        norms[0] = 0.0
        norms[1] = 0.0

    for s in range(tokens // SEQ):
        rows = slice(s * SEQ, (s + 1) * SEQ)
        for p in range(QUAD // PAIR):
            lanes = pl.ds(pl.multiple_of(step * QUAD + p * PAIR, PAIR), PAIR)
            pair = q_ref[rows, lanes]
            grad = jnp.zeros((SEQ, PAIR), f32)
            for h in range(PAIR // HD):
                unit = step * (QUAD // HD) + p * (PAIR // HD) + h
                grad = grad + dot(ds_ref[unit, rows, :], only_head(pair, h))
            gks[rows, p * PAIR : (p + 1) * PAIR] = grad.astype(bf16)
    grad = dot(ft_ref[...], gks[...]) * in_scale
    w = w_ref[...]
    u = lamb_direction(w, m_ref[...], s_ref[...], grad)
    u_all[:, cols] = u
    w_all[:, cols] = w
    norms[0] += jnp.sum(w * w)
    norms[1] += jnp.sum(u * u)

    @pl.when(step == last)
    def _():
        ratio = lamb_ratio(norms)
        new = lambda here: w_all[here, :] - ratio * u_all[here, :]
        turned_ref[:TURN] = turn_ref[...]
        keys = width // 2 - LAST
        mines = ((turned_ref.at[TURN:], keys), (mine_ref, LAST))
        deal(new, width, mines, ((turned_other, keys), (other_ref, LAST)))


SCALARS = pl.BlockSpec(memory_space=pltpu.SMEM)
STAYS = pl.BlockSpec(memory_space=pltpu.VMEM)


def in_hbm(*xs):
    return [pltpu.with_memory_space_constraint(x, pltpu.HBM) for x in xs]


def in_vmem(*xs):
    return [pltpu.with_memory_space_constraint(x, pltpu.VMEM) for x in xs]


def query_step(members, f, v, o, wq, wk, m, s):
    tokens, width = f.shape
    heads = wq.shape[1]
    tok = pl.BlockSpec((tokens, QUAD), lambda i: (0, i))
    mat = pl.BlockSpec((width, QUAD), lambda i: (0, i))
    full = pl.BlockSpec((tokens, width), lambda i: (0, 0))
    shapes = [(FIRST, heads), (TURN, heads), (width // 2 + NOTE, heads), (NOTE, heads)]
    return pl.pallas_call(
        query_kernel,
        grid=(heads // QUAD,),
        in_specs=[SCALARS, full, tok, tok, mat, mat, mat, mat],
        out_specs=[STAYS] * 7,
        out_shape=[pltpu.VMEM(x, f32) for x in shapes]
        + [pltpu.VMEM(x, bf16) for x in ((heads // HD, tokens, SEQ), (tokens, heads), (width, tokens))],
        scratch_shapes=[
            pltpu.VMEM((tokens, QUAD), bf16),
            pltpu.VMEM((QUAD, tokens), bf16),
            pltpu.VMEM((QUAD, tokens), bf16),
            pltpu.VMEM((width, heads), f32),
            pltpu.VMEM((width, heads), f32),
            pltpu.SMEM((2,), f32),
            pltpu.VMEM((QUAD, tokens), bf16),
            pltpu.VMEM((QUAD, tokens), bf16),
        ],
        compiler_params=pltpu.CompilerParams(vmem_limit_bytes=36 << 20),
        name="query_step",
    )(*in_hbm(members, f, v, o, wq, wk, m, s))


def key_step(ds, q, ft, turn, w, m, s):
    tokens, heads = q.shape
    width = ft.shape[0]
    keys = width // 2 - LAST
    mat = pl.BlockSpec((width, QUAD), lambda i: (0, i))
    return pl.pallas_call(
        key_kernel,
        grid=(heads // QUAD,),
        in_specs=[STAYS] * 4 + [mat, mat, mat],
        out_specs=[STAYS] * 4,
        out_shape=[pltpu.VMEM((r, heads), f32) for r in (TURN + keys, LAST, keys, LAST)],
        scratch_shapes=[
            pltpu.VMEM((tokens, QUAD), bf16),
            pltpu.VMEM((width, heads), f32),
            pltpu.VMEM((width, heads), f32),
            pltpu.SMEM((2,), f32),
        ],
        compiler_params=pltpu.CompilerParams(vmem_limit_bytes=24 << 20),
        name="key_step",
    )(*in_vmem(ds, q, ft, turn), *in_hbm(w, m, s))


A_ME, B_ME, A_MATE, B_MATE, A_CHIP, A_COUNT, B_COUNT, B_COUNT_MATE = range(8)
DISTANCES = (2, 1, 3)
NO_HBM = pl.CostEstimate(flops=0, transcendentals=0, bytes_accessed=0)


def small_call(kernel, name, shapes, *operands):
    got = pl.pallas_call(
        kernel,
        in_specs=[STAYS] * len(operands),
        out_specs=[STAYS] * len(shapes),
        out_shape=[pltpu.VMEM(s, f32) for s in shapes],
        compiler_params=pltpu.CompilerParams(vmem_limit_bytes=8 << 20),
        cost_estimate=NO_HBM,
        name=name,
    )(*in_vmem(*operands))
    return list(got)


def row(facts, i):
    return facts[i : i + 1, :]


def chip_sum(mine, theirs, facts):
    rows, width = mine.shape

    def kernel(mine_ref, theirs_ref, facts_ref, out_ref, facts_out):
        f = facts_ref[...]
        got = theirs_ref[theirs_ref.shape[0] - NOTE :]
        at = lax.broadcasted_iota(jnp.int32, f.shape, 0)
        f = jnp.where(at == A_MATE, row(got, 0), jnp.where(at == B_MATE, row(got, 1), f))
        f = jnp.where(at == A_CHIP, row(f, A_ME) + row(f, A_MATE), f)
        out_ref[rows:] = f
        facts_out[...] = f
        out_ref[:rows] = row(f, A_ME) * mine_ref[...] + row(f, A_MATE) * theirs_ref[:rows]

    return small_call(kernel, "chip_sum", [(rows + NOTE, width), facts.shape], mine, theirs, facts)


def chip_sum_turned(turned, theirs_query, theirs_key, facts):
    rows, width = turned.shape

    def kernel(turned_ref, tq_ref, tk_ref, facts_ref, out_ref, theirs_out):
        f = facts_ref[...]
        theirs_out[:TURN] = tq_ref[FIRST : FIRST + TURN]
        theirs_out[TURN:] = tk_ref[...]
        out_ref[...] = row(f, A_ME) * turned_ref[...] + row(f, A_MATE) * theirs_out[...]

    shapes = [(rows, width), (rows, width)]
    return small_call(kernel, "chip_sum_turned", shapes, turned, theirs_query, theirs_key, facts)


def chip_sum_last(mine, theirs, facts):
    rows, width = mine.shape

    def kernel(mine_ref, theirs_ref, facts_ref, out_ref):
        f = facts_ref[...]
        out_ref[...] = row(f, A_ME) * mine_ref[...] + row(f, A_MATE) * theirs_ref[...]

    return small_call(kernel, "chip_sum_last", [(rows, width)], mine, theirs, facts)[0]


def row_mean(mine, theirs, far, facts, first):
    rows, width = mine.shape
    piece = rows // GROUP

    def kernel(mine_ref, theirs_ref, far_ref, facts_ref, own, s2, s1, s3, held, held_mate, *maybe_facts):
        f = facts_ref[...]
        if first:
            at = lax.broadcasted_iota(jnp.int32, f.shape, 0)
            count = row(f, A_CHIP) + row(far_ref[rows : rows + NOTE], A_CHIP)
            f = jnp.where(at == A_COUNT, jnp.maximum(count, 1.0), f)
            maybe_facts[0][...] = f
        y = ring_at()
        for d, out in enumerate((own, s1, s2, s3)):
            here = pl.ds(pl.multiple_of((y + d) % GROUP * piece, 8), piece)
            m, t = mine_ref[here, :], theirs_ref[here, :]
            mean = (row(f, A_ME) * m + row(f, A_MATE) * t + far_ref[here, :]) / row(f, A_COUNT)
            m = jnp.where(row(f, A_ME) > 0, mean, m)
            t = jnp.where(row(f, A_MATE) > 0, mean, t)
            held[here, :] = m
            held_mate[here, :] = t
            out[:piece] = m * row(f, B_ME)
            out[piece:] = t * row(f, B_MATE)

    shapes = [(2 * piece, width)] * 4 + [(rows, width)] * 2
    if first:
        shapes = shapes + [facts.shape]
    got = small_call(kernel, "row_mean", shapes, mine, theirs, far, facts)
    return got if first else got + [facts]


def col_sum(own, got, facts):
    rows, width = own.shape

    def kernel(own_ref, g1, g2, g3, facts_ref, out):
        out[:rows] = own_ref[...] + g1[...] + g2[...] + g3[...]
        out[rows:] = facts_ref[...]

    return small_call(kernel, "col_sum", [(rows + NOTE, width)], own, *got, facts)[0]


def col_mean(own, got, facts, split=False):
    rows, width = own.shape
    piece = rows // 2

    def kernel(own_ref, g1, g2, g3, facts_ref, *outs):
        f = facts_ref[...]
        total = own_ref[...] + g1[...] + g2[...] + g3[...]
        mate = outs[1] if split else outs[0].at[piece:]
        outs[0][:piece] = total[:piece] / row(f, B_COUNT)
        mate[...] = total[piece:] / row(f, B_COUNT_MATE)

    shapes = [(piece, width)] * 2 if split else [(rows, width)]
    return small_call(kernel, "col_mean", shapes, own, *got, facts)


def joined(me, mate):
    piece, width = me.shape

    def kernel(me_ref, mate_ref, out):
        out[:piece] = me_ref[...]
        out[piece:] = mate_ref[...]

    return small_call(kernel, "joined", [(2 * piece, width)], me, mate)[0]


def choose(held, held_mate, p0, p3, p1, p2, facts, first):
    rows, width = held.shape
    piece = rows // GROUP

    def kernel(held_ref, held_mate_ref, b0, b3, b1, b2, facts_ref, me, mate, *maybe_facts):
        f = facts_ref[...]
        if first:
            notes = [b[2 * piece :] for b in (b1, b2, b3)]
            count = sum([row(n, B_ME) for n in notes], row(f, B_ME))
            count_mate = sum([row(n, B_MATE) for n in notes], row(f, B_MATE))
            over, over_mate = jnp.maximum(count, 1.0), jnp.maximum(count_mate, 1.0)
            at = lax.broadcasted_iota(jnp.int32, f.shape, 0)
            maybe_facts[0][...] = jnp.where(at == B_COUNT, over, jnp.where(at == B_COUNT_MATE, over_mate, f))
        for d, src in enumerate((b0, b1, b2, b3)):
            here = pl.ds(pl.multiple_of((ring_at() + GROUP - d) % GROUP * piece, 8), piece)
            mine, theirs = src[:piece], src[piece : 2 * piece]
            if first:
                mine, theirs = mine / over, theirs / over_mate
            me[here, :] = jnp.where(row(f, B_ME) > 0, mine, held_ref[here, :])
            mate[here, :] = jnp.where(row(f, B_MATE) > 0, theirs, held_mate_ref[here, :])

    shapes = [(rows, width)] * 2 + ([facts.shape] if first else [])
    return small_call(kernel, "choose", shapes, held, held_mate, p0, p3, p1, p2, facts)


def place(size, mine, other, turned, turned_other):
    width = mine.shape[1]

    def kernel(mine_ref, other_ref, turned_ref, turned_other_ref, out_ref, sems):
        copies = []
        for a, b, side in ((mine_ref, turned_ref, core_at()), (other_ref, turned_other_ref, 1 - core_at())):
            for src, skip, count in ((a, 0, FIRST), (b, FIRST, TURN)):
                to = out_ref.at[pl.ds(pl.multiple_of(side * (size // 2) + skip, 8), count), :]
                copies.append(pltpu.make_async_copy(src.at[:count], to, sems.at[len(copies)]))
                copies[-1].start()
        for copy in copies:
            copy.wait()

    return pl.pallas_call(
        kernel,
        in_specs=[STAYS] * 4,
        out_specs=pl.BlockSpec(memory_space=pl.ANY),
        out_shape=jax.ShapeDtypeStruct((size, width), f32),
        scratch_shapes=[pltpu.SemaphoreType.DMA((4,))],
        name="place",
    )(*in_vmem(mine, other, turned, turned_other))


def finish(size, turned, turned_other, held, held_mate, p0, p2, p3, p1, facts):
    rows, width = held.shape
    piece = rows // GROUP
    blocks = 2 * GROUP
    keys = size // 2 - rows

    def kernel(turned_ref, turned_other_ref, held_ref, mate_ref, b0, b2, b3, b1, facts_ref, out_ref, made, sems):
        takes = row(facts_ref[...], B_ME) > 0
        y = ring_at()
        copies = []
        sides = ((core_at(), turned_ref, held_ref), (1 - core_at(), turned_other_ref, mate_ref))
        for side, (whose, early, kept) in enumerate(sides):
            base = whose * (size // 2)
            to = out_ref.at[pl.ds(pl.multiple_of(base, 8), keys), :]
            copies.append(pltpu.make_async_copy(early.at[TURN:], to, sems.at[len(copies)]))
            copies[-1].start()
            for d, src in enumerate((b0, b1, b2, b3)):
                at = pl.multiple_of((y + GROUP - d) % GROUP * piece, 8)
                block = side * GROUP + d
                made[block] = jnp.where(takes, src[side * piece : (side + 1) * piece], kept[pl.ds(at, piece), :])
                to = out_ref.at[pl.ds(pl.multiple_of(base + keys + at, 8), piece), :]
                copies.append(pltpu.make_async_copy(made.at[block], to, sems.at[len(copies)]))
                copies[-1].start()
        for copy in copies:
            copy.wait()

    return pl.pallas_call(
        kernel,
        in_specs=[STAYS] * 9,
        out_specs=pl.BlockSpec(memory_space=pl.ANY),
        out_shape=jax.ShapeDtypeStruct((size, width), f32),
        scratch_shapes=[pltpu.VMEM((blocks, piece, width), f32), pltpu.SemaphoreType.DMA((blocks + 2,))],
        compiler_params=pltpu.CompilerParams(vmem_limit_bytes=8 << 20),
        name="finish",
    )(*in_vmem(turned, turned_other, held, held_mate, p0, p2, p3, p1, facts))


def ring(step):
    size = lax.axis_size("col")
    return [(i, i - i % GROUP + (i + step) % GROUP) for i in range(size)]


def swap(bit):
    return [(i, i ^ bit) for i in range(lax.axis_size("row"))]


def to_mate(x):
    return lax.ppermute(x, "row", swap(1))


def to_far(x):
    return lax.ppermute(x, "row", swap(2))


def around(x2, x1, x3):
    return [lax.ppermute(x, "col", ring(d)) for d, x in zip(DISTANCES, (x2, x1, x3))]


def after(x, *done):
    return lax.optimization_barrier((x, *done))[0]


def per_device(features, values, out_grad, query_weight, key_weight, query_mean, query_square, key_mean, key_square, members):
    f, v, o, wq, wk = [a[0, 0] for a in (features, values, out_grad, query_weight, key_weight)]
    mq, sq, mk, sk = [a[0, 0] for a in (query_mean, query_square, key_mean, key_square)]

    size = wq.shape[0]
    mine0, turn, other0, facts, ds, queries, ft = query_step(members, f, v, o, wq, wk, mq, sq)
    theirs0 = to_mate(other0)
    part0, facts = chip_sum(mine0, theirs0, facts)
    far0 = to_far(part0)
    mine1, mine2, other1, other2 = key_step(after(ds, part0), queries, ft, turn, wk, mk, sk)
    part1, theirs1 = chip_sum_turned(mine1, theirs0, to_mate(other1), facts)
    far1 = to_far(after(part1, far0))
    theirs2 = to_mate(after(other2, far0))
    part2 = chip_sum_last(mine2, theirs2, facts)
    far2 = to_far(after(part2, far1))

    own0, s2, s1, s3, held0, held_mate0, facts = row_mean(mine0, theirs0, far0, facts, True)
    total0 = col_sum(own0, around(s2, s1, s3), facts)
    p2, p1, p3 = around(total0, total0, total0)
    me0, mate0, counted = choose(held0, held_mate0, total0, p3, p1, p2, facts, True)
    other0 = to_mate(mate0)

    own1, s2, s1, s3, held1, held_mate1, _ = row_mean(mine1, theirs1, after(far1, total0), facts, False)
    got1 = around(s2, s1, s3)
    total1 = col_mean(after(own1, me0), got1, counted)[0]
    p2, p1, p3 = around(total1, total1, total1)
    me1, mate1 = choose(held1, held_mate1, total1, p3, p1, p2, facts, False)
    other1 = to_mate(mate1)

    own2, s2, s1, s3, held2, held_mate2, _ = row_mean(mine2, theirs2, after(far2, total1), facts, False)
    got2 = around(s2, s1, s3)
    held_mate2 = to_mate(held_mate2)
    me2, mate2 = col_mean(after(own2, me1), got2, counted, split=True)
    total2 = joined(me2, to_mate(mate2))
    p2, p1, p3 = around(total2, total2, total2)
    query = place(size, me0, other0, me1, other1)
    key = finish(size, me1, other1, held2, held_mate2, total2, after(p2, query), p3, p1, facts)
    return query[None, None], key[None, None]


def solution(mesh):
    mats = P("row", "col", None, None)
    return jax.shard_map(
        per_device,
        mesh=mesh,
        in_specs=(mats,) * 9 + (P("row", "col", None),),
        out_specs=(mats, mats),
        check_vma=False,
    )
```
